256 devices in a mesh: dp: 4 (over x_lo, core), ctx: 64 (over x_hi, z, y).
Axes of the slice: x: 4 (x_hi: 2, x_lo: 2; x = x_hi * 2 + x_lo), y: 4, z: 8, core: 2. Of those that a mesh axis runs over, the one named last changes fastest.
Arguments:
- query_gate: bfloat16 [8192, 4096], P('ctx', 'dp'), may hold values from -6 to 6
- key_gate: bfloat16 [8192, 4096], P('ctx', 'dp'), may hold values from -6 to 6
- value_gate: bfloat16 [8192, 4096], P('ctx', 'dp'), may hold values from -6 to 6
- out_grad: bfloat16 [8192, 4096], P('ctx', 'dp'), may hold values from -6 to 6
- filter_taps: float32 [8192, 4096], P('ctx', 'dp'), may hold values from -0.0625 to 0.0625
- skip: float32 [4096], P('dp'), may hold values from -6 to 6
Outputs:
- grad_query: bfloat16 [8192, 4096], P('ctx', 'dp')
- grad_key: bfloat16 [8192, 4096], P('ctx', 'dp')
- grad_value: bfloat16 [8192, 4096], P('ctx', 'dp')
- grad_filter: float32 [8192, 4096], P('ctx', 'dp')
- grad_skip: float32 [4096], P('dp')
The draws below stay inside these ranges and needn't reach their ends.
All inputs are finite; a program needn't handle non-finite values.
Results may differ from the reference program's by a relative error of at most 0.001.
Values sent between devices are 32-bit elements; how exact they have to be, the bound alone decides.
A program may use at most 64 MiB of HBM per device.

```python
import math
import jax
import jax.numpy as jnp
from jax import lax

C = 4096
LEN = 8192


def steps_of(own_key, shape, cuts, least, top_value):
    factor_of = 1.0
    for axis_at, blocks in cuts:
        heights = jax.random.uniform(jax.random.fold_in(jax.random.fold_in(own_key, 6), axis_at), (blocks,), jnp.float32, least / len(cuts), top_value / len(cuts))
        factor_of = factor_of * jnp.repeat(jnp.exp(heights), shape[axis_at] // blocks).reshape((-1,) + (1,) * (len(shape) - 1 - axis_at))
    return factor_of


def centred(rng, shape, scale, reach, shards=(), kind=jnp.bfloat16):
    loudness = steps_of(rng, shape, shards, -0.22, 0.18) if shards else 1.0
    values = jax.random.normal(rng, shape, jnp.float32) * scale * loudness
    return jnp.minimum(jnp.maximum(values, -reach), reach).astype(kind)


def setup_inputs(seed: int = 0) -> dict:
    seeds = jax.random.split(jax.random.key(seed), 7)
    return {
        "query_gate": centred(seeds[0], (LEN, C), 1.0, 6.0, ((0, 64), (1, 4))),
        "key_gate": centred(seeds[1], (LEN, C), 1.0, 6.0, ((0, 64), (1, 4))),
        "value_gate": centred(seeds[2], (LEN, C), 1.0, 6.0, ((0, 64), (1, 4))),
        "out_grad": centred(seeds[3], (LEN, C), 1.0, 6.0, ((0, 64), (1, 4))),
        "filter_taps": centred(seeds[4], (LEN, C), (LEN ** -0.5), 0.0625, ((0, 64), (1, 4)), jnp.float32),
        "skip": centred(seeds[5], (C,), 1.0, 6.0, ((0, 4),), jnp.float32),
    }


def reference(query_gate, key_gate, value_gate, out_grad, filter_taps, skip):
    width_block = math.gcd(C, 512)
    block_count = C // width_block

    def split(values):
        return values.reshape(LEN, block_count, width_block).transpose(1, 0, 2)

    def merge(values):
        return values.transpose(1, 0, 2).reshape(LEN, C)

    def one_block(inputs):
        query_vals, key_vals, value_vals, grads, filt, skip_part = inputs
        key_vals = key_vals.astype(jnp.float32)
        value_vals = value_vals.astype(jnp.float32)
        grads = grads.astype(jnp.float32)
        gated = key_vals * value_vals
        grad_conv = grads * query_vals.astype(jnp.float32)
        filter_spec = jnp.fft.rfft(filt, n=2 * LEN, axis=0)
        gated_spec = jnp.fft.rfft(gated, n=2 * LEN, axis=0)
        conv_spec = jnp.fft.rfft(grad_conv, n=2 * LEN, axis=0)
        conv_time = jnp.fft.irfft(filter_spec * gated_spec, n=2 * LEN, axis=0)[:LEN]
        back_time = jnp.fft.irfft(jnp.conj(filter_spec) * conv_spec, n=2 * LEN, axis=0)[:LEN]
        corr_time = jnp.fft.irfft(jnp.conj(gated_spec) * conv_spec, n=2 * LEN, axis=0)[:LEN]
        conv_full = conv_time + skip_part[None, :] * gated
        grad_query = (grads * conv_full).astype(jnp.bfloat16)
        back_full = back_time + skip_part[None, :] * grad_conv
        grad_key = (back_full * value_vals).astype(jnp.bfloat16)
        grad_value = (back_full * key_vals).astype(jnp.bfloat16)
        return (grad_query, grad_key, grad_value, corr_time, lax.optimization_barrier(jnp.sum(grad_conv * gated, axis=0)))
    grad_query, grad_key, grad_value, corr_all, skip_terms = lax.map(one_block, (split(query_gate), split(key_gate), split(value_gate), split(out_grad), split(filter_taps), skip.reshape(block_count, width_block)))
    root_scale = 1.0 / math.sqrt(LEN)
    grad_filter = merge(corr_all) * root_scale
    grad_skip = skip_terms.reshape(C) * root_scale
    return (merge(grad_query), merge(grad_key), merge(grad_value), grad_filter, grad_skip)
```

```python
import functools
import math

import jax
import jax.numpy as jnp
import ml_dtypes
import numpy as np
from jax import lax
from jax.experimental import pallas as pl
from jax.experimental.pallas import tpu as pltpu
from jax.sharding import PartitionSpec as P

MESH = pl.DeviceIdType.MESH
BLOCKS = 64
LANES = 128
WIDTH = 1024
OWN = WIDTH // BLOCKS
PERIOD = 2 * BLOCKS * LANES
HALF = 72
GROUP = 4
ROWS = GROUP * HALF
Z_ORDER = (1, 7, 3, 5, 2, 6, 4, 0)


def split_bf16(values):
    high = values.astype(ml_dtypes.bfloat16)
    low = (values - high.astype(np.float64)).astype(ml_dtypes.bfloat16)
    return high, low


@functools.cache
def tables():
    k1 = np.arange(HALF)[:, None]
    valid = (k1 <= BLOCKS).astype(np.float64)
    block = np.arange(BLOCKS)[None, :]
    angle = 2 * np.pi * ((k1 * block) % (2 * BLOCKS)) / (2 * BLOCKS)
    fwd_block = np.concatenate([np.cos(angle) * valid, -np.sin(angle) * valid])
    high, low = split_bf16(fwd_block)
    fwd_block = np.concatenate([high, high, low, low], axis=1)
    weight = np.where((k1 == 0) | (k1 == BLOCKS), 1.0, 2.0) * valid / PERIOD
    inv_block = np.concatenate([np.cos(angle) * weight, -np.sin(angle) * weight]).T
    inv_high, inv_low = split_bf16(inv_block)
    pad = np.zeros((BLOCKS, 256 - 2 * HALF), ml_dtypes.bfloat16)
    inv_block = np.concatenate(
        [np.concatenate([inv_high, pad], 1), np.concatenate([inv_low, pad], 1)]
    )
    ids = np.arange(LANES)
    local = 2 * np.pi * ((ids[:, None] * ids[None, :]) % LANES) / LANES
    cos, sin = np.cos(local), np.sin(local)
    fwd_local = np.block([[cos, -sin], [sin, cos]])
    inv_local = np.block([[cos, sin], [-sin, cos]])
    matrices = np.concatenate([fwd_block, *split_bf16(fwd_local), *split_bf16(inv_local), inv_block])
    twist = 2 * np.pi * ((k1 * ids[None, :]) % PERIOD) / PERIOD
    twists = np.concatenate([np.cos(twist), np.sin(twist)]).astype(np.float32)
    return matrices, twists


FWD_BLOCK = 0
FWD_HIGH = 2 * HALF
FWD_LOW = FWD_HIGH + 256
INV_HIGH = FWD_LOW + 256
INV_LOW = INV_HIGH + 256
INV_BLOCK = INV_LOW + 256


def halves(values):
    high = values.astype(jnp.bfloat16)
    return high, (values - high.astype(jnp.float32)).astype(jnp.bfloat16)


def dot(left, right):
    return jnp.dot(left, right, preferred_element_type=jnp.float32)


def kernel(
    query_hbm, key_hbm, value_hbm, grads_hbm, taps_hbm, skip_hbm, mats_hbm, twists_hbm,
    gq_hbm, gk_hbm, gv_hbm, gf_hbm, gs_hbm,
    query, key, value, grads, taps, skip, mats, twists,
    gq, gk, gv, gf, gs,
    leaving, landed, spectra, rows_out, rows_in,
    load_sems, store_sems, send_sems, recv_sems,
):
    me = lax.axis_index("ctx")
    dp = lax.axis_index("dp")
    my_x, my_z, my_y = me // 32, (me // 4) % 8, me % 4

    loads = [
        pltpu.make_async_copy(src, dst, load_sems.at[i])
        for i, (src, dst) in enumerate(
            ((taps_hbm, taps), (key_hbm, key), (value_hbm, value), (grads_hbm, grads),
             (query_hbm, query), (twists_hbm, twists), (mats_hbm, mats), (skip_hbm, skip))
        )
    ]
    for load in loads:
        load.start()

    barrier = pltpu.get_barrier_semaphore()

    def greet(i, carry):
        there = lax.rem(me + 1 + i, BLOCKS)
        pl.semaphore_signal(barrier, inc=1, device_id=(dp, there), device_id_type=MESH)
        return carry

    lax.fori_loop(0, BLOCKS - 1, greet, 0)

    def rows_of(device):
        return pl.ds(pl.multiple_of(device * OWN, OWN), OWN)

    def to_all(send_one):
        def body(j, carry):
            for zi, dz in enumerate(Z_ORDER):
                xy = (j + zi) % 8 if dz else j
                there = ((my_x + xy // 4) % 2) * 32 + ((my_z + dz) % 8) * 4 + (my_y + xy) % 4
                if dz:
                    send_one(there)
                else:
                    @pl.when(j > 0)
                    def _():
                        send_one(there)
            return carry

        lax.fori_loop(0, 8, body, 0)

    def send_signal(s):
        def one(there):
            pltpu.make_async_remote_copy(
                src_ref=leaving.at[s, rows_of(there), :],
                dst_ref=landed.at[s, rows_of(me), :],
                send_sem=send_sems.at[s],
                recv_sem=recv_sems.at[s],
                device_id=(dp, there),
                device_id_type=MESH,
            ).start()

        to_all(one)
        landed[s, rows_of(me), :] = leaving[s, rows_of(me), :]

    def wait_bytes(s, sems):
        most = pl.ds(0, (BLOCKS - 1) * OWN)
        pltpu.make_async_copy(leaving.at[s, most, :], landed.at[s, most, :], sems.at[s]).wait()

    def columns(j):
        return slice(j * LANES, (j + 1) * LANES)

    loads[0].wait()
    for j in range(WIDTH // LANES):
        leaving[0, columns(j), :] = taps[:, columns(j)].T
    pl.semaphore_wait(barrier, BLOCKS - 1)
    send_signal(0)

    loads[1].wait()
    loads[2].wait()
    for j in range(WIDTH // LANES):
        gated = key[:, columns(j)].astype(jnp.float32) * value[:, columns(j)].astype(jnp.float32)
        leaving[1, columns(j), :] = gated.T
    send_signal(1)

    loads[3].wait()
    loads[4].wait()
    for j in range(WIDTH // LANES):
        conv_grad = grads[:, columns(j)].astype(jnp.float32) * query[:, columns(j)].astype(jnp.float32)
        leaving[2, columns(j), :] = conv_grad.T
    send_signal(2)

    for load in loads[5:]:
        load.wait()

    def forward(s):
        signal = landed.at[s]
        cos_twist, sin_twist = twists[0:HALF, :], twists[HALF:, :]
        for group in range(OWN // GROUP):
            lines = []
            for pair in range(GROUP // 2):
                first = group * GROUP + 2 * pair
                both = jnp.concatenate(
                    [signal[pl.ds(first + i, BLOCKS, stride=OWN), :] for i in range(2)], axis=1
                )
                high, low = halves(both)
                stacked = jnp.concatenate([high, low, high, low], axis=0)
                parts = dot(mats[FWD_BLOCK : FWD_BLOCK + 2 * HALF, :], stacked)
                for i in range(2):
                    real, imag = parts[:HALF, columns(i)], parts[HALF:, columns(i)]
                    lines.append(
                        jnp.concatenate(
                            [real * cos_twist + imag * sin_twist, imag * cos_twist - real * sin_twist],
                            axis=1,
                        )
                    )
            high, low = halves(jnp.concatenate(lines, axis=0))
            spectra[s, group * ROWS : (group + 1) * ROWS, :] = (
                dot(high, mats[FWD_HIGH : FWD_HIGH + 256, :])
                + dot(low, mats[FWD_HIGH : FWD_HIGH + 256, :])
                + dot(high, mats[FWD_LOW : FWD_LOW + 256, :])
            )

    def inverse(s, left, right, conjugate):
        result = leaving.at[3 + s]
        cos_twist, sin_twist = twists[0:HALF, :], twists[HALF:, :]
        for group in range(OWN // GROUP):
            rows = slice(group * ROWS, (group + 1) * ROWS)
            a_re, a_im = spectra[left, rows, 0:LANES], spectra[left, rows, LANES:]
            b_re, b_im = spectra[right, rows, 0:LANES], spectra[right, rows, LANES:]
            if conjugate:
                product = [a_re * b_re + a_im * b_im, a_re * b_im - a_im * b_re]
            else:
                product = [a_re * b_re - a_im * b_im, a_re * b_im + a_im * b_re]
            high, low = halves(jnp.concatenate(product, axis=1))
            back = (
                dot(high, mats[INV_HIGH : INV_HIGH + 256, :])
                + dot(low, mats[INV_HIGH : INV_HIGH + 256, :])
                + dot(high, mats[INV_LOW : INV_LOW + 256, :])
            )
            for pair in range(GROUP // 2):
                pieces = []
                for i in range(2):
                    top = (2 * pair + i) * HALF
                    real, imag = back[top : top + HALF, 0:LANES], back[top : top + HALF, LANES:]
                    pieces.append(
                        jnp.concatenate(
                            [real * cos_twist - imag * sin_twist, real * sin_twist + imag * cos_twist],
                            axis=0,
                        )
                    )
                high, low = halves(jnp.concatenate(pieces, axis=1))
                inv_high = mats[INV_BLOCK : INV_BLOCK + BLOCKS, 0 : 2 * HALF]
                inv_low = mats[INV_BLOCK + BLOCKS : INV_BLOCK + 2 * BLOCKS, 0 : 2 * HALF]
                values = dot(inv_high, high) + dot(inv_high, low) + dot(inv_low, high)
                first = group * GROUP + 2 * pair
                for i in range(2):
                    result[pl.ds(first + i, BLOCKS, stride=OWN), :] = values[:, columns(i)]

    wait_bytes(0, recv_sems)
    forward(0)
    wait_bytes(1, recv_sems)
    forward(1)
    inverse(0, 0, 1, False)
    send_signal(3)
    wait_bytes(2, recv_sems)
    forward(2)
    inverse(1, 0, 2, True)
    send_signal(4)
    inverse(2, 1, 2, True)
    send_signal(5)

    total = jnp.zeros((OWN, LANES), jnp.float32)
    for b in range(BLOCKS):
        total = total + landed[1, b * OWN : (b + 1) * OWN, :] * landed[2, b * OWN : (b + 1) * OWN, :]
    total = jnp.sum(total, axis=1, keepdims=True)
    lane = lax.broadcasted_iota(jnp.int32, (OWN, LANES), 1)
    channel = lax.broadcasted_iota(jnp.int32, (OWN, LANES), 0)
    placed = jnp.where(lane == channel + (me % 8) * OWN, total, 0.0)
    root_scale = 1.0 / math.sqrt(BLOCKS * LANES)
    rows_out[...] = jnp.sum(placed, axis=0, keepdims=True) * root_scale
    rows_in[pl.ds(me, 1)] = rows_out[...].reshape(1, 1, LANES)

    def send_row(there):
        pltpu.make_async_remote_copy(
            src_ref=rows_out,
            dst_ref=rows_in.at[me],
            send_sem=send_sems.at[6],
            recv_sem=recv_sems.at[6],
            device_id=(dp, there),
            device_id_type=MESH,
        ).start()

    to_all(send_row)

    wait_bytes(3, recv_sems)
    for j in range(WIDTH // LANES):
        gated = key[:, columns(j)].astype(jnp.float32) * value[:, columns(j)].astype(jnp.float32)
        conv = landed[3, columns(j), :].T + skip[:, columns(j)] * gated
        gq[:, columns(j)] = (grads[:, columns(j)].astype(jnp.float32) * conv).astype(jnp.bfloat16)
    stores = [pltpu.make_async_copy(gq, gq_hbm, store_sems.at[0])]
    stores[0].start()

    wait_bytes(4, recv_sems)
    for j in range(WIDTH // LANES):
        conv_grad = grads[:, columns(j)].astype(jnp.float32) * query[:, columns(j)].astype(jnp.float32)
        back = landed[4, columns(j), :].T + skip[:, columns(j)] * conv_grad
        gk[:, columns(j)] = (back * value[:, columns(j)].astype(jnp.float32)).astype(jnp.bfloat16)
        gv[:, columns(j)] = (back * key[:, columns(j)].astype(jnp.float32)).astype(jnp.bfloat16)
    for i, (src, dst) in enumerate(((gk, gk_hbm), (gv, gv_hbm))):
        stores.append(pltpu.make_async_copy(src, dst, store_sems.at[1 + i]))
        stores[-1].start()

    wait_bytes(5, recv_sems)
    for j in range(WIDTH // LANES):
        gf[:, columns(j)] = landed[5, columns(j), :].T * root_scale
    stores.append(pltpu.make_async_copy(gf, gf_hbm, store_sems.at[3]))
    stores[-1].start()

    most = pl.ds(0, BLOCKS - 1)
    pltpu.make_async_copy(rows_in.at[most], rows_in.at[most], recv_sems.at[6]).wait()
    gs[...] = jnp.sum(rows_in[...].reshape(8, 8, LANES), axis=1)
    stores.append(pltpu.make_async_copy(gs, gs_hbm, store_sems.at[4]))
    stores[-1].start()

    for s in range(6):
        wait_bytes(s, send_sems)
    pltpu.make_async_copy(rows_in.at[most], rows_in.at[most], send_sems.at[6]).wait()
    for store in stores:
        store.wait()


def on_device(query_gate, key_gate, value_gate, out_grad, filter_taps, skip):
    matrices, twists = tables()
    shape = query_gate.shape
    assert shape == (LANES, WIDTH) and lax.axis_size("ctx") == BLOCKS
    bf16, f32 = jnp.bfloat16, jnp.float32
    outs = pl.pallas_call(
        kernel,
        out_shape=[
            jax.ShapeDtypeStruct(shape, bf16),
            jax.ShapeDtypeStruct(shape, bf16),
            jax.ShapeDtypeStruct(shape, bf16),
            jax.ShapeDtypeStruct(shape, f32),
            jax.ShapeDtypeStruct((8, LANES), f32),
        ],
        in_specs=[pl.BlockSpec(memory_space=pl.ANY)] * 8,
        out_specs=[pl.BlockSpec(memory_space=pl.ANY)] * 5,
        scratch_shapes=[
            *[pltpu.VMEM(shape, bf16)] * 4,
            pltpu.VMEM(shape, f32),
            pltpu.VMEM((1, WIDTH), f32),
            pltpu.VMEM(matrices.shape, bf16),
            pltpu.VMEM(twists.shape, f32),
            *[pltpu.VMEM(shape, bf16)] * 3,
            pltpu.VMEM(shape, f32),
            pltpu.VMEM((8, LANES), f32),
            pltpu.VMEM((6, WIDTH, LANES), f32),
            pltpu.VMEM((6, WIDTH, LANES), f32),
            pltpu.VMEM((3, OWN * HALF, 2 * LANES), f32),
            pltpu.VMEM((1, LANES), f32),
            pltpu.VMEM((BLOCKS, 1, LANES), f32),
            pltpu.SemaphoreType.DMA((8,)),
            pltpu.SemaphoreType.DMA((5,)),
            pltpu.SemaphoreType.DMA((7,)),
            pltpu.SemaphoreType.DMA((7,)),
        ],
        compiler_params=pltpu.CompilerParams(
            collective_id=0, has_side_effects=True, vmem_limit_bytes=48 << 20
        ),
        cost_estimate=pl.CostEstimate(
            flops=4 * 10**9, bytes_accessed=3 * 10**6, transcendentals=0
        ),
        name="hyena_backward",
    )(
        query_gate, key_gate, value_gate, out_grad, filter_taps, skip.reshape(1, WIDTH),
        jnp.asarray(matrices), jnp.asarray(twists),
    )
    return (*outs[:4], outs[4].reshape(WIDTH))


def solution(mesh):
    return jax.shard_map(
        on_device,
        mesh=mesh,
        in_specs=(*[P("ctx", "dp")] * 5, P("dp")),
        out_specs=(*[P("ctx", "dp")] * 4, P("dp")),
        check_vma=False,
    )
```

```python
import functools
import math

import jax
import jax.numpy as jnp
import numpy as np
from jax import lax
from jax.experimental import pallas as pl
from jax.experimental.pallas import tpu as pltpu
from jax.sharding import PartitionSpec as P

MESH = pl.DeviceIdType.MESH
BLOCKS = 64
LANES = 128
WIDTH = 1024
OWN = WIDTH // BLOCKS
PERIOD = 2 * BLOCKS * LANES
HALF = 72
GROUP = 4
ROWS = GROUP * HALF
Z_ORDER = (1, 7, 3, 5, 2, 6, 4, 0)


@functools.cache
def tables():
    k1 = np.arange(HALF)[:, None]
    valid = (k1 <= BLOCKS).astype(np.float64)
    block = np.arange(BLOCKS)[None, :]
    angle = 2 * np.pi * ((k1 * block) % (2 * BLOCKS)) / (2 * BLOCKS)
    fwd_block = np.concatenate([np.cos(angle) * valid, -np.sin(angle) * valid])
    fwd_block = np.concatenate([fwd_block] * 4, axis=1)
    weight = np.where((k1 == 0) | (k1 == BLOCKS), 1.0, 2.0) * valid / PERIOD
    inv_block = np.concatenate([np.cos(angle) * weight, -np.sin(angle) * weight]).T
    inv_block = np.pad(inv_block, ((0, 0), (0, 256 - 2 * HALF)))
    ids = np.arange(LANES)
    local = 2 * np.pi * ((ids[:, None] * ids[None, :]) % LANES) / LANES
    cos, sin = np.cos(local), np.sin(local)
    fwd_local = np.block([[cos, -sin], [sin, cos]])
    inv_local = np.block([[cos, sin], [-sin, cos]])
    matrices = np.concatenate([fwd_block, fwd_local, inv_local, inv_block]).astype(np.float32)
    twist = 2 * np.pi * ((k1 * ids[None, :]) % PERIOD) / PERIOD
    twists = np.concatenate([np.cos(twist), np.sin(twist)]).astype(np.float32)
    return matrices, twists


FWD_BLOCK = slice(0, 2 * HALF)
FWD_LOCAL = slice(2 * HALF, 2 * HALF + 256)
INV_LOCAL = slice(2 * HALF + 256, 2 * HALF + 512)
INV_BLOCK = slice(2 * HALF + 512, 2 * HALF + 512 + BLOCKS)
MATRIX_ROWS = INV_BLOCK.stop


def halves(values):
    high = values.astype(jnp.bfloat16)
    return high, (values - high.astype(jnp.float32)).astype(jnp.bfloat16)


def dot(left, right):
    return jnp.dot(left, right, preferred_element_type=jnp.float32)


def kernel(
    query_hbm, key_hbm, value_hbm, grads_hbm, taps_hbm, skip_hbm, mats_hbm, twists_hbm,
    gq_hbm, gk_hbm, gv_hbm, gf_hbm, gs_hbm,
    query, key, value, grads, taps, skip, mats, mats_high, mats_low, twists,
    gq, gk, gv, gf, gs,
    leaving, landed, spectra, rows_out, rows_in,
    load_sems, store_sems, send_sems, recv_sems,
):
    me = lax.axis_index("ctx")
    dp = lax.axis_index("dp")
    my_x, my_z, my_y = me // 32, (me // 4) % 8, me % 4

    loads = [
        pltpu.make_async_copy(src, dst, load_sems.at[i])
        for i, (src, dst) in enumerate(
            ((taps_hbm, taps), (key_hbm, key), (value_hbm, value), (grads_hbm, grads),
             (query_hbm, query), (twists_hbm, twists), (mats_hbm, mats), (skip_hbm, skip))
        )
    ]
    for load in loads:
        load.start()

    barrier = pltpu.get_barrier_semaphore()

    def greet(i, carry):
        there = lax.rem(me + 1 + i, BLOCKS)
        pl.semaphore_signal(barrier, inc=1, device_id=(dp, there), device_id_type=MESH)
        return carry

    lax.fori_loop(0, BLOCKS - 1, greet, 0)

    def rows_of(device):
        return pl.ds(pl.multiple_of(device * OWN, OWN), OWN)

    def to_all(send_one):
        def body(j, carry):
            for zi, dz in enumerate(Z_ORDER):
                xy = (j + zi) % 8 if dz else j
                there = ((my_x + xy // 4) % 2) * 32 + ((my_z + dz) % 8) * 4 + (my_y + xy) % 4
                if dz:
                    send_one(there)
                else:
                    @pl.when(j > 0)
                    def _():
                        send_one(there)
            return carry

        lax.fori_loop(0, 8, body, 0)

    def send_signal(s):
        def one(there):
            pltpu.make_async_remote_copy(
                src_ref=leaving.at[s, rows_of(there), :],
                dst_ref=landed.at[s, rows_of(me), :],
                send_sem=send_sems.at[s],
                recv_sem=recv_sems.at[s],
                device_id=(dp, there),
                device_id_type=MESH,
            ).start()

        to_all(one)
        landed[s, rows_of(me), :] = leaving[s, rows_of(me), :]

    def wait_bytes(s, sems):
        most = pl.ds(0, (BLOCKS - 1) * OWN)
        pltpu.make_async_copy(leaving.at[s, most, :], landed.at[s, most, :], sems.at[s]).wait()

    def columns(j):
        return slice(j * LANES, (j + 1) * LANES)

    loads[0].wait()
    for j in range(WIDTH // LANES):
        leaving[0, columns(j), :] = taps[:, columns(j)].T
    pl.semaphore_wait(barrier, BLOCKS - 1)
    send_signal(0)

    loads[1].wait()
    loads[2].wait()
    for j in range(WIDTH // LANES):
        gated = key[:, columns(j)].astype(jnp.float32) * value[:, columns(j)].astype(jnp.float32)
        leaving[1, columns(j), :] = gated.T
    send_signal(1)

    loads[3].wait()
    loads[4].wait()
    for j in range(WIDTH // LANES):
        conv_grad = grads[:, columns(j)].astype(jnp.float32) * query[:, columns(j)].astype(jnp.float32)
        leaving[2, columns(j), :] = conv_grad.T
    send_signal(2)

    for load in loads[5:]:
        load.wait()
    mats_high[...], mats_low[...] = halves(mats[...])
    half_lanes = 2 * BLOCKS
    fwd_block = jnp.concatenate(
        [mats_high[FWD_BLOCK, :half_lanes], mats_low[FWD_BLOCK, half_lanes:]], axis=1
    )

    def forward(s):
        signal = landed.at[s]
        cos_twist, sin_twist = twists[0:HALF, :], twists[HALF:, :]
        for group in range(OWN // GROUP):
            lines = []
            for pair in range(GROUP // 2):
                first = group * GROUP + 2 * pair
                both = jnp.concatenate(
                    [signal[pl.ds(first + i, BLOCKS, stride=OWN), :] for i in range(2)], axis=1
                )
                high, low = halves(both)
                stacked = jnp.concatenate([high, low, high, low], axis=0)
                parts = dot(fwd_block, stacked)
                for i in range(2):
                    real, imag = parts[:HALF, columns(i)], parts[HALF:, columns(i)]
                    lines.append(
                        jnp.concatenate(
                            [real * cos_twist + imag * sin_twist, imag * cos_twist - real * sin_twist],
                            axis=1,
                        )
                    )
            high, low = halves(jnp.concatenate(lines, axis=0))
            spectra[s, group * ROWS : (group + 1) * ROWS, :] = (
                dot(high, mats_high[FWD_LOCAL, :])
                + dot(low, mats_high[FWD_LOCAL, :])
                + dot(high, mats_low[FWD_LOCAL, :])
            )

    def inverse(s, left, right, conjugate):
        result = leaving.at[3 + s]
        cos_twist, sin_twist = twists[0:HALF, :], twists[HALF:, :]
        for group in range(OWN // GROUP):
            rows = slice(group * ROWS, (group + 1) * ROWS)
            a_re, a_im = spectra[left, rows, 0:LANES], spectra[left, rows, LANES:]
            b_re, b_im = spectra[right, rows, 0:LANES], spectra[right, rows, LANES:]
            if conjugate:
                product = [a_re * b_re + a_im * b_im, a_re * b_im - a_im * b_re]
            else:
                product = [a_re * b_re - a_im * b_im, a_re * b_im + a_im * b_re]
            high, low = halves(jnp.concatenate(product, axis=1))
            back = (
                dot(high, mats_high[INV_LOCAL, :])
                + dot(low, mats_high[INV_LOCAL, :])
                + dot(high, mats_low[INV_LOCAL, :])
            )
            for pair in range(GROUP // 2):
                pieces = []
                for i in range(2):
                    top = (2 * pair + i) * HALF
                    real, imag = back[top : top + HALF, 0:LANES], back[top : top + HALF, LANES:]
                    pieces.append(
                        jnp.concatenate(
                            [real * cos_twist - imag * sin_twist, real * sin_twist + imag * cos_twist],
                            axis=0,
                        )
                    )
                high, low = halves(jnp.concatenate(pieces, axis=1))
                inv_high = mats_high[INV_BLOCK, 0 : 2 * HALF]
                inv_low = mats_low[INV_BLOCK, 0 : 2 * HALF]
                values = dot(inv_high, high) + dot(inv_high, low) + dot(inv_low, high)
                first = group * GROUP + 2 * pair
                for i in range(2):
                    result[pl.ds(first + i, BLOCKS, stride=OWN), :] = values[:, columns(i)]

    wait_bytes(0, recv_sems)
    forward(0)
    wait_bytes(1, recv_sems)
    forward(1)
    inverse(0, 0, 1, False)
    send_signal(3)
    wait_bytes(2, recv_sems)
    forward(2)
    inverse(1, 0, 2, True)
    send_signal(4)
    inverse(2, 1, 2, True)
    send_signal(5)

    total = jnp.zeros((OWN, LANES), jnp.float32)
    for b in range(BLOCKS):
        total = total + landed[1, b * OWN : (b + 1) * OWN, :] * landed[2, b * OWN : (b + 1) * OWN, :]
    total = jnp.sum(total, axis=1, keepdims=True)
    lane = lax.broadcasted_iota(jnp.int32, (OWN, LANES), 1)
    channel = lax.broadcasted_iota(jnp.int32, (OWN, LANES), 0)
    placed = jnp.where(lane == channel + (me % 8) * OWN, total, 0.0)
    root_scale = 1.0 / math.sqrt(BLOCKS * LANES)
    rows_out[...] = jnp.sum(placed, axis=0, keepdims=True) * root_scale
    rows_in[pl.ds(me, 1)] = rows_out[...].reshape(1, 1, LANES)

    def send_row(there):
        pltpu.make_async_remote_copy(
            src_ref=rows_out,
            dst_ref=rows_in.at[me],
            send_sem=send_sems.at[6],
            recv_sem=recv_sems.at[6],
            device_id=(dp, there),
            device_id_type=MESH,
        ).start()

    to_all(send_row)

    wait_bytes(3, recv_sems)
    for j in range(WIDTH // LANES):
        gated = key[:, columns(j)].astype(jnp.float32) * value[:, columns(j)].astype(jnp.float32)
        conv = landed[3, columns(j), :].T + skip[:, columns(j)] * gated
        gq[:, columns(j)] = (grads[:, columns(j)].astype(jnp.float32) * conv).astype(jnp.bfloat16)
    stores = [pltpu.make_async_copy(gq, gq_hbm, store_sems.at[0])]
    stores[0].start()

    wait_bytes(4, recv_sems)
    for j in range(WIDTH // LANES):
        conv_grad = grads[:, columns(j)].astype(jnp.float32) * query[:, columns(j)].astype(jnp.float32)
        back = landed[4, columns(j), :].T + skip[:, columns(j)] * conv_grad
        gk[:, columns(j)] = (back * value[:, columns(j)].astype(jnp.float32)).astype(jnp.bfloat16)
        gv[:, columns(j)] = (back * key[:, columns(j)].astype(jnp.float32)).astype(jnp.bfloat16)
    for i, (src, dst) in enumerate(((gk, gk_hbm), (gv, gv_hbm))):
        stores.append(pltpu.make_async_copy(src, dst, store_sems.at[1 + i]))
        stores[-1].start()

    wait_bytes(5, recv_sems)
    for j in range(WIDTH // LANES):
        gf[:, columns(j)] = landed[5, columns(j), :].T * root_scale
    stores.append(pltpu.make_async_copy(gf, gf_hbm, store_sems.at[3]))
    stores[-1].start()

    most = pl.ds(0, BLOCKS - 1)
    pltpu.make_async_copy(rows_in.at[most], rows_in.at[most], recv_sems.at[6]).wait()
    gs[...] = jnp.sum(rows_in[...].reshape(8, 8, LANES), axis=1)
    stores.append(pltpu.make_async_copy(gs, gs_hbm, store_sems.at[4]))
    stores[-1].start()

    for s in range(6):
        wait_bytes(s, send_sems)
    pltpu.make_async_copy(rows_in.at[most], rows_in.at[most], send_sems.at[6]).wait()
    for store in stores:
        store.wait()


def hand_over(*refs):
    given, taken, held, in_sems, out_sems = refs[:5], refs[5:10], refs[10:15], refs[15], refs[16]
    reads = [pltpu.make_async_copy(given[i], held[i], in_sems.at[i]) for i in range(5)]
    writes = [pltpu.make_async_copy(held[i], taken[i], out_sems.at[i]) for i in range(5)]
    for read in reads:
        read.start()
    for read, write in zip(reads, writes, strict=True):
        read.wait()
        write.start()
    for write in writes:
        write.wait()


def on_device(query_gate, key_gate, value_gate, out_grad, filter_taps, skip):
    matrices, twists = tables()
    shape = query_gate.shape
    assert shape == (LANES, WIDTH) and lax.axis_size("ctx") == BLOCKS
    bf16, f32 = jnp.bfloat16, jnp.float32
    out_shape = [
        jax.ShapeDtypeStruct(shape, bf16),
        jax.ShapeDtypeStruct(shape, bf16),
        jax.ShapeDtypeStruct(shape, bf16),
        jax.ShapeDtypeStruct(shape, f32),
        jax.ShapeDtypeStruct((8, LANES), f32),
    ]
    outs = pl.pallas_call(
        kernel,
        out_shape=out_shape,
        in_specs=[pl.BlockSpec(memory_space=pl.ANY)] * 8,
        out_specs=[pl.BlockSpec(memory_space=pl.ANY)] * 5,
        scratch_shapes=[
            *[pltpu.VMEM(shape, bf16)] * 4,
            pltpu.VMEM(shape, f32),
            pltpu.VMEM((1, WIDTH), f32),
            pltpu.VMEM(matrices.shape, f32),
            *[pltpu.VMEM(matrices.shape, bf16)] * 2,
            pltpu.VMEM(twists.shape, f32),
            *[pltpu.VMEM(shape, bf16)] * 3,
            pltpu.VMEM(shape, f32),
            pltpu.VMEM((8, LANES), f32),
            pltpu.VMEM((6, WIDTH, LANES), f32),
            pltpu.VMEM((6, WIDTH, LANES), f32),
            pltpu.VMEM((3, OWN * HALF, 2 * LANES), f32),
            pltpu.VMEM((1, LANES), f32),
            pltpu.VMEM((BLOCKS, 1, LANES), f32),
            pltpu.SemaphoreType.DMA((8,)),
            pltpu.SemaphoreType.DMA((5,)),
            pltpu.SemaphoreType.DMA((7,)),
            pltpu.SemaphoreType.DMA((7,)),
        ],
        compiler_params=pltpu.CompilerParams(
            collective_id=0, has_side_effects=True, vmem_limit_bytes=63 << 20
        ),
        cost_estimate=pl.CostEstimate(
            flops=4 * 10**9, bytes_accessed=3 * 10**6, transcendentals=0
        ),
        name="hyena_backward",
    )(
        query_gate, key_gate, value_gate, out_grad, filter_taps, skip.reshape(1, WIDTH),
        jnp.asarray(matrices), jnp.asarray(twists),
    )
    outs = pl.pallas_call(
        hand_over,
        out_shape=out_shape,
        in_specs=[pl.BlockSpec(memory_space=pl.ANY)] * 5,
        out_specs=[pl.BlockSpec(memory_space=pl.ANY)] * 5,
        scratch_shapes=[
            *[pltpu.VMEM(out.shape, out.dtype) for out in out_shape],
            pltpu.SemaphoreType.DMA((5,)),
            pltpu.SemaphoreType.DMA((5,)),
        ],
        compiler_params=pltpu.CompilerParams(vmem_limit_bytes=63 << 20),
        cost_estimate=pl.CostEstimate(flops=0, bytes_accessed=3 * 10**6, transcendentals=0),
        name="hand_over",
    )(*outs)
    return (*outs[:4], outs[4].reshape(WIDTH))


def solution(mesh):
    return jax.shard_map(
        on_device,
        mesh=mesh,
        in_specs=(*[P("ctx", "dp")] * 5, P("dp")),
        out_specs=(*[P("ctx", "dp")] * 4, P("dp")),
        check_vma=False,
    )
```

```python
import functools
import math

import jax
import jax.numpy as jnp
import numpy as np
from jax import lax
from jax.experimental import pallas as pl
from jax.experimental.pallas import tpu as pltpu
from jax.sharding import PartitionSpec as P

MESH = pl.DeviceIdType.MESH
BLOCKS = 64
LANES = 128
WIDTH = 1024
OWN = WIDTH // BLOCKS
PERIOD = 2 * BLOCKS * LANES
HALF = 72
GROUP = 4
ROWS = GROUP * HALF
Z_ORDER = (1, 7, 3, 5, 2, 6, 4, 0)


@functools.cache
def tables():
    k1 = np.arange(HALF)[:, None]
    valid = (k1 <= BLOCKS).astype(np.float64)
    block = np.arange(BLOCKS)[None, :]
    angle = 2 * np.pi * ((k1 * block) % (2 * BLOCKS)) / (2 * BLOCKS)
    fwd_block = np.concatenate([np.cos(angle) * valid, -np.sin(angle) * valid])
    fwd_block = np.concatenate([fwd_block] * 4, axis=1)
    weight = np.where((k1 == 0) | (k1 == BLOCKS), 1.0, 2.0) * valid / PERIOD
    inv_block = np.concatenate([np.cos(angle) * weight, -np.sin(angle) * weight]).T
    inv_block = np.pad(inv_block, ((0, 0), (0, 256 - 2 * HALF)))
    ids = np.arange(LANES)
    local = 2 * np.pi * ((ids[:, None] * ids[None, :]) % LANES) / LANES
    cos, sin = np.cos(local), np.sin(local)
    fwd_local = np.block([[cos, -sin], [sin, cos]])
    inv_local = np.block([[cos, sin], [-sin, cos]])
    matrices = np.concatenate([fwd_block, fwd_local, inv_local, inv_block]).astype(np.float32)
    twist = 2 * np.pi * ((k1 * ids[None, :]) % PERIOD) / PERIOD
    twists = np.concatenate([np.cos(twist), np.sin(twist)]).astype(np.float32)
    return matrices, twists


FWD_BLOCK = slice(0, 2 * HALF)
FWD_LOCAL = slice(2 * HALF, 2 * HALF + 256)
INV_LOCAL = slice(2 * HALF + 256, 2 * HALF + 512)
INV_BLOCK = slice(2 * HALF + 512, 2 * HALF + 512 + BLOCKS)
MATRIX_ROWS = INV_BLOCK.stop


def halves(values):
    high = values.astype(jnp.bfloat16)
    return high, (values - high.astype(jnp.float32)).astype(jnp.bfloat16)


def dot(left, right):
    return jnp.dot(left, right, preferred_element_type=jnp.float32)


def kernel(
    query_hbm, key_hbm, value_hbm, grads_hbm, taps_hbm, skip_hbm, mats_hbm, twists_hbm,
    gq, gk, gv, gf, gs,
    query, key, value, grads, taps, skip, mats, mats_high, mats_low, twists,
    leaving, landed, spectra, rows_out, rows_in,
    load_sems, send_sems, recv_sems, row_send_sems, row_recv_sems,
):
    me = lax.axis_index("ctx")
    dp = lax.axis_index("dp")
    my_x, my_z, my_y = me // 32, (me // 4) % 8, me % 4

    loads = [
        pltpu.make_async_copy(src, dst, load_sems.at[i])
        for i, (src, dst) in enumerate(
            ((taps_hbm, taps), (key_hbm, key), (value_hbm, value), (grads_hbm, grads),
             (query_hbm, query), (twists_hbm, twists), (mats_hbm, mats), (skip_hbm, skip))
        )
    ]
    loads[0].start()

    barrier = pltpu.get_barrier_semaphore()
    planes = [((my_z + dz) % 8) * 4 for dz in range(8)]
    spots = [((my_x + xy // 4) % 2) * 32 + (my_y + xy) % 4 for xy in range(8)]
    for dz in (4, 3, 5, 2, 6, 1, 7, 0):
        for xy in (6, 5, 7, 4, 2, 1, 3, 0):
            if dz or xy:
                pl.semaphore_signal(
                    barrier, inc=1, device_id=(dp, planes[dz] + spots[xy]), device_id_type=MESH
                )
    for load in loads[1:]:
        load.start()

    def rows_of(device):
        return pl.ds(pl.multiple_of(device * OWN, OWN), OWN)

    def to_all(send_one):
        def body(j, carry):
            for zi, dz in enumerate(Z_ORDER):
                xy = (j + zi) % 8 if dz else j
                there = ((my_x + xy // 4) % 2) * 32 + ((my_z + dz) % 8) * 4 + (my_y + xy) % 4
                if dz:
                    send_one(there)
                else:
                    @pl.when(j > 0)
                    def _():
                        send_one(there)
            return carry

        lax.fori_loop(0, 8, body, 0)

    def send_signal(s):
        def one(there):
            pltpu.make_async_remote_copy(
                src_ref=leaving.at[s, rows_of(there), :],
                dst_ref=landed.at[s, rows_of(me), :],
                send_sem=send_sems.at[s],
                recv_sem=recv_sems.at[s],
                device_id=(dp, there),
                device_id_type=MESH,
            ).start()

        to_all(one)
        landed[s, rows_of(me), :] = leaving[s, rows_of(me), :]

    def wait_bytes(s, sems):
        most = pl.ds(0, (BLOCKS - 1) * OWN)
        pltpu.make_async_copy(leaving.at[s, most, :], landed.at[s, most, :], sems.at[s]).wait()

    def columns(j):
        return slice(j * LANES, (j + 1) * LANES)

    loads[0].wait()
    for j in range(WIDTH // LANES):
        leaving[0, columns(j), :] = taps[:, columns(j)].T
    pl.semaphore_wait(barrier, BLOCKS - 1)
    send_signal(0)

    my_row, my_group = me % 8, me // 8
    root_scale = 1.0 / math.sqrt(BLOCKS * LANES)

    def send_rows(step, source_of, device_of, slot):
        for i in range(1, 8):
            pltpu.make_async_remote_copy(
                src_ref=source_of(i),
                dst_ref=rows_in.at[step, slot],
                send_sem=row_send_sems.at[step],
                recv_sem=row_recv_sems.at[step],
                device_id=(dp, device_of(i)),
                device_id_type=MESH,
            ).start()

    def wait_rows(step, sems):
        most = pl.ds(0, 7)
        pltpu.make_async_copy(rows_in.at[step, most], rows_in.at[step, most], sems.at[step]).wait()

    def in_group(i):
        return my_group * 8 + (my_row + i) % 8

    def across(i):
        return ((my_group + i) % 8) * 8 + my_row

    for load in loads[1:5]:
        load.wait()
    for j in range(WIDTH // LANES):
        gated = key[:, columns(j)].astype(jnp.float32) * value[:, columns(j)].astype(jnp.float32)
        conv_grad = grads[:, columns(j)].astype(jnp.float32) * query[:, columns(j)].astype(jnp.float32)
        rows_out[j] = jnp.sum(gated * conv_grad, axis=0, keepdims=True)
    send_rows(0, lambda i: rows_out.at[(my_row + i) % 8], in_group, my_row)
    rows_in[0, pl.ds(my_row, 1)] = rows_out[pl.ds(my_row, 1)]

    for j in range(WIDTH // LANES):
        gated = key[:, columns(j)].astype(jnp.float32) * value[:, columns(j)].astype(jnp.float32)
        leaving[1, columns(j), :] = gated.T
    send_signal(1)

    for j in range(WIDTH // LANES):
        conv_grad = grads[:, columns(j)].astype(jnp.float32) * query[:, columns(j)].astype(jnp.float32)
        leaving[2, columns(j), :] = conv_grad.T
    send_signal(2)

    for load in loads[5:]:
        load.wait()
    mats_high[...], mats_low[...] = halves(mats[...])
    half_lanes = 2 * BLOCKS
    fwd_block = jnp.concatenate(
        [mats_high[FWD_BLOCK, :half_lanes], mats_low[FWD_BLOCK, half_lanes:]], axis=1
    )

    def forward(s):
        signal = landed.at[s]
        cos_twist, sin_twist = twists[0:HALF, :], twists[HALF:, :]
        for group in range(OWN // GROUP):
            lines = []
            for pair in range(GROUP // 2):
                first = group * GROUP + 2 * pair
                both = jnp.concatenate(
                    [signal[pl.ds(first + i, BLOCKS, stride=OWN), :] for i in range(2)], axis=1
                )
                high, low = halves(both)
                stacked = jnp.concatenate([high, low, high, low], axis=0)
                parts = dot(fwd_block, stacked)
                for i in range(2):
                    real, imag = parts[:HALF, columns(i)], parts[HALF:, columns(i)]
                    lines.append(
                        jnp.concatenate(
                            [real * cos_twist + imag * sin_twist, imag * cos_twist - real * sin_twist],
                            axis=1,
                        )
                    )
            high, low = halves(jnp.concatenate(lines, axis=0))
            spectra[s, group * ROWS : (group + 1) * ROWS, :] = (
                dot(high, mats_high[FWD_LOCAL, :])
                + dot(low, mats_high[FWD_LOCAL, :])
                + dot(high, mats_low[FWD_LOCAL, :])
            )

    def inverse(s, left, right, conjugate):
        result = leaving.at[3 + s]
        cos_twist, sin_twist = twists[0:HALF, :], twists[HALF:, :]
        for group in range(OWN // GROUP):
            rows = slice(group * ROWS, (group + 1) * ROWS)
            a_re, a_im = spectra[left, rows, 0:LANES], spectra[left, rows, LANES:]
            b_re, b_im = spectra[right, rows, 0:LANES], spectra[right, rows, LANES:]
            if conjugate:
                product = [a_re * b_re + a_im * b_im, a_re * b_im - a_im * b_re]
            else:
                product = [a_re * b_re - a_im * b_im, a_re * b_im + a_im * b_re]
            high, low = halves(jnp.concatenate(product, axis=1))
            back = (
                dot(high, mats_high[INV_LOCAL, :])
                + dot(low, mats_high[INV_LOCAL, :])
                + dot(high, mats_low[INV_LOCAL, :])
            )
            for pair in range(GROUP // 2):
                pieces = []
                for i in range(2):
                    top = (2 * pair + i) * HALF
                    real, imag = back[top : top + HALF, 0:LANES], back[top : top + HALF, LANES:]
                    pieces.append(
                        jnp.concatenate(
                            [real * cos_twist - imag * sin_twist, real * sin_twist + imag * cos_twist],
                            axis=0,
                        )
                    )
                high, low = halves(jnp.concatenate(pieces, axis=1))
                inv_high = mats_high[INV_BLOCK, 0 : 2 * HALF]
                inv_low = mats_low[INV_BLOCK, 0 : 2 * HALF]
                values = dot(inv_high, high) + dot(inv_high, low) + dot(inv_low, high)
                first = group * GROUP + 2 * pair
                for i in range(2):
                    result[pl.ds(first + i, BLOCKS, stride=OWN), :] = values[:, columns(i)]

    wait_bytes(0, recv_sems)
    forward(0)
    wait_rows(0, row_recv_sems)
    rows_out[8] = jnp.sum(rows_in[0], axis=0)
    send_rows(1, lambda i: rows_out.at[8], across, my_group)
    rows_in[1, pl.ds(my_group, 1)] = rows_out[pl.ds(8, 1)]

    wait_bytes(1, recv_sems)
    forward(1)
    inverse(0, 0, 1, False)
    send_signal(3)

    wait_bytes(2, recv_sems)
    wait_rows(1, row_recv_sems)
    rows_out[9] = jnp.sum(rows_in[1], axis=0) * root_scale
    send_rows(2, lambda i: rows_out.at[9], in_group, my_row)
    rows_in[2, pl.ds(my_row, 1)] = rows_out[pl.ds(9, 1)]
    forward(2)
    inverse(1, 0, 2, True)
    send_signal(4)
    inverse(2, 1, 2, True)
    send_signal(5)

    wait_bytes(3, recv_sems)
    for j in range(WIDTH // LANES):
        gated = key[:, columns(j)].astype(jnp.float32) * value[:, columns(j)].astype(jnp.float32)
        conv = landed[3, columns(j), :].T + skip[:, columns(j)] * gated
        gq[:, columns(j)] = (grads[:, columns(j)].astype(jnp.float32) * conv).astype(jnp.bfloat16)
    wait_rows(2, row_recv_sems)
    for j in range(8):
        gs[j : j + 1, :] = rows_in[2, j]

    wait_bytes(4, recv_sems)
    for j in range(WIDTH // LANES):
        conv_grad = grads[:, columns(j)].astype(jnp.float32) * query[:, columns(j)].astype(jnp.float32)
        back = landed[4, columns(j), :].T + skip[:, columns(j)] * conv_grad
        gk[:, columns(j)] = (back * value[:, columns(j)].astype(jnp.float32)).astype(jnp.bfloat16)
        gv[:, columns(j)] = (back * key[:, columns(j)].astype(jnp.float32)).astype(jnp.bfloat16)

    wait_bytes(5, recv_sems)
    for j in range(WIDTH // LANES):
        gf[:, columns(j)] = landed[5, columns(j), :].T * root_scale

    for s in range(6):
        wait_bytes(s, send_sems)
    for step in range(3):
        wait_rows(step, row_send_sems)


def hand_over(*refs):
    given, taken, sems = refs[:5], refs[5:10], refs[10]
    writes = [pltpu.make_async_copy(given[i], taken[i], sems.at[i]) for i in range(5)]
    for write in writes:
        write.start()
    for write in writes:
        write.wait()


def on_device(query_gate, key_gate, value_gate, out_grad, filter_taps, skip):
    matrices, twists = tables()
    shape = query_gate.shape
    assert shape == (LANES, WIDTH) and lax.axis_size("ctx") == BLOCKS
    bf16, f32 = jnp.bfloat16, jnp.float32
    out_shape = [
        jax.ShapeDtypeStruct(shape, bf16),
        jax.ShapeDtypeStruct(shape, bf16),
        jax.ShapeDtypeStruct(shape, bf16),
        jax.ShapeDtypeStruct(shape, f32),
        jax.ShapeDtypeStruct((8, LANES), f32),
    ]
    outs = pl.pallas_call(
        kernel,
        out_shape=[pltpu.VMEM(out.shape, out.dtype) for out in out_shape],
        in_specs=[pl.BlockSpec(memory_space=pl.ANY)] * 8,
        out_specs=[pl.BlockSpec(memory_space=pltpu.VMEM)] * 5,
        scratch_shapes=[
            *[pltpu.VMEM(shape, bf16)] * 4,
            pltpu.VMEM(shape, f32),
            pltpu.VMEM((1, WIDTH), f32),
            pltpu.VMEM(matrices.shape, f32),
            *[pltpu.VMEM(matrices.shape, bf16)] * 2,
            pltpu.VMEM(twists.shape, f32),
            pltpu.VMEM((6, WIDTH, LANES), f32),
            pltpu.VMEM((6, WIDTH, LANES), f32),
            pltpu.VMEM((3, OWN * HALF, 2 * LANES), f32),
            pltpu.VMEM((10, 1, LANES), f32),
            pltpu.VMEM((3, 8, 1, LANES), f32),
            pltpu.SemaphoreType.DMA((8,)),
            pltpu.SemaphoreType.DMA((6,)),
            pltpu.SemaphoreType.DMA((6,)),
            pltpu.SemaphoreType.DMA((3,)),
            pltpu.SemaphoreType.DMA((3,)),
        ],
        compiler_params=pltpu.CompilerParams(
            collective_id=0, has_side_effects=True, vmem_limit_bytes=40 << 20
        ),
        cost_estimate=pl.CostEstimate(
            flops=4 * 10**9, bytes_accessed=3 * 10**6, transcendentals=0
        ),
        name="hyena_backward",
    )(
        *[
            pltpu.with_memory_space_constraint(operand, pltpu.HBM)
            for operand in (
                query_gate, key_gate, value_gate, out_grad, filter_taps, skip.reshape(1, WIDTH),
                jnp.asarray(matrices), jnp.asarray(twists),
            )
        ]
    )
    outs = pl.pallas_call(
        hand_over,
        out_shape=[pltpu.HBM(out.shape, out.dtype) for out in out_shape],
        in_specs=[pl.BlockSpec(memory_space=pl.ANY)] * 5,
        out_specs=[pl.BlockSpec(memory_space=pl.ANY)] * 5,
        scratch_shapes=[pltpu.SemaphoreType.DMA((5,))],
        compiler_params=pltpu.CompilerParams(vmem_limit_bytes=8 << 20),
        cost_estimate=pl.CostEstimate(flops=0, bytes_accessed=3 * 10**6, transcendentals=0),
        name="hand_over",
    )(*[pltpu.with_memory_space_constraint(out, pltpu.VMEM) for out in outs])
    return (*outs[:4], outs[4].reshape(WIDTH))


def solution(mesh):
    return jax.shard_map(
        on_device,
        mesh=mesh,
        in_specs=(*[P("ctx", "dp")] * 5, P("dp")),
        out_specs=(*[P("ctx", "dp")] * 4, P("dp")),
        check_vma=False,
    )
```

```python
import functools
import math

import jax
import jax.numpy as jnp
import numpy as np
from jax import lax
from jax.experimental import pallas as pl
from jax.experimental.pallas import tpu as pltpu
from jax.sharding import PartitionSpec as P

MESH = pl.DeviceIdType.MESH
BLOCKS = 64
LANES = 128
WIDTH = 1024
OWN = WIDTH // BLOCKS
PERIOD = 2 * BLOCKS * LANES
HALF = 72
GROUP = 4
ROWS = GROUP * HALF
Z_ORDER = (1, 7, 3, 5, 2, 6, 4, 0)


@functools.cache
def tables():
    k1 = np.arange(HALF)[:, None]
    valid = (k1 <= BLOCKS).astype(np.float64)
    block = np.arange(BLOCKS)[None, :]
    angle = 2 * np.pi * ((k1 * block) % (2 * BLOCKS)) / (2 * BLOCKS)
    fwd_block = np.concatenate([np.cos(angle) * valid, -np.sin(angle) * valid])
    fwd_block = np.pad(fwd_block, ((0, 0), (0, 256 - BLOCKS)))
    weight = np.where((k1 == 0) | (k1 == BLOCKS), 1.0, 2.0) * valid / PERIOD
    inv_block = np.concatenate([np.cos(angle) * weight, -np.sin(angle) * weight]).T
    inv_block = np.pad(inv_block, ((0, 0), (0, 256 - 2 * HALF)))
    ids = np.arange(LANES)
    local = 2 * np.pi * ((ids[:, None] * ids[None, :]) % LANES) / LANES
    cos, sin = np.cos(local), np.sin(local)
    fwd_local = np.block([[cos, -sin], [sin, cos]])
    inv_local = np.block([[cos, sin], [-sin, cos]])
    matrices = np.concatenate([fwd_block, fwd_local, inv_local, inv_block]).astype(np.float32)
    twist = 2 * np.pi * ((k1 * ids[None, :]) % PERIOD) / PERIOD
    twists = np.concatenate([np.cos(twist), np.sin(twist)]).astype(np.float32)
    return matrices, twists


FWD_BLOCK = slice(0, 2 * HALF)
FWD_LOCAL = slice(2 * HALF, 2 * HALF + 256)
INV_LOCAL = slice(2 * HALF + 256, 2 * HALF + 512)
INV_BLOCK = slice(2 * HALF + 512, 2 * HALF + 512 + BLOCKS)


def dot(left, right):
    return jnp.dot(
        left, right, precision=lax.Precision.HIGHEST, preferred_element_type=jnp.float32
    )


def kernel(
    query_hbm, key_hbm, value_hbm, grads_hbm, taps_hbm, skip_hbm, mats_hbm, twists_hbm,
    gq, gk, gv, gf, gs,
    query, key, value, grads, taps, skip, mats, twists,
    leaving, landed, spectra, rows_out, rows_in,
    load_sems, send_sems, recv_sems, row_send_sems, row_recv_sems,
):
    me = lax.axis_index("ctx")
    dp = lax.axis_index("dp")
    my_x, my_z, my_y = me // 32, (me // 4) % 8, me % 4

    loads = [
        pltpu.make_async_copy(src, dst, load_sems.at[i])
        for i, (src, dst) in enumerate(
            ((taps_hbm, taps), (key_hbm, key), (value_hbm, value), (grads_hbm, grads),
             (query_hbm, query), (twists_hbm, twists), (mats_hbm, mats), (skip_hbm, skip))
        )
    ]
    loads[0].start()

    barrier = pltpu.get_barrier_semaphore()
    planes = [((my_z + dz) % 8) * 4 for dz in range(8)]
    spots = [((my_x + xy // 4) % 2) * 32 + (my_y + xy) % 4 for xy in range(8)]
    for dz in (4, 3, 5, 2, 6, 1, 7, 0):
        for xy in (6, 5, 7, 4, 2, 1, 3, 0):
            if dz or xy:
                pl.semaphore_signal(
                    barrier, inc=1, device_id=(dp, planes[dz] + spots[xy]), device_id_type=MESH
                )
    for load in loads[1:]:
        load.start()

    def rows_of(device):
        return pl.ds(pl.multiple_of(device * OWN, OWN), OWN)

    def to_all(send_one):
        def body(j, carry):
            for zi, dz in enumerate(Z_ORDER):
                xy = (j + zi) % 8 if dz else j
                there = ((my_x + xy // 4) % 2) * 32 + ((my_z + dz) % 8) * 4 + (my_y + xy) % 4
                if dz:
                    send_one(there)
                else:
                    @pl.when(j > 0)
                    def _():
                        send_one(there)
            return carry

        lax.fori_loop(0, 8, body, 0)

    def send_signal(s):
        def one(there):
            pltpu.make_async_remote_copy(
                src_ref=leaving.at[s, rows_of(there), :],
                dst_ref=landed.at[s, rows_of(me), :],
                send_sem=send_sems.at[s],
                recv_sem=recv_sems.at[s],
                device_id=(dp, there),
                device_id_type=MESH,
            ).start()

        to_all(one)
        landed[s, rows_of(me), :] = leaving[s, rows_of(me), :]

    def wait_bytes(s, sems):
        most = pl.ds(0, (BLOCKS - 1) * OWN)
        pltpu.make_async_copy(leaving.at[s, most, :], landed.at[s, most, :], sems.at[s]).wait()

    def columns(j):
        return slice(j * LANES, (j + 1) * LANES)

    loads[0].wait()
    for j in range(WIDTH // LANES):
        leaving[0, columns(j), :] = taps[:, columns(j)].T
    pl.semaphore_wait(barrier, BLOCKS - 1)
    send_signal(0)

    my_row, my_group = me % 8, me // 8
    root_scale = 1.0 / math.sqrt(BLOCKS * LANES)

    def send_rows(step, source_of, device_of, slot):
        for i in range(1, 8):
            pltpu.make_async_remote_copy(
                src_ref=source_of(i),
                dst_ref=rows_in.at[step, slot],
                send_sem=row_send_sems.at[step],
                recv_sem=row_recv_sems.at[step],
                device_id=(dp, device_of(i)),
                device_id_type=MESH,
            ).start()

    def wait_rows(step, sems):
        most = pl.ds(0, 7)
        pltpu.make_async_copy(rows_in.at[step, most], rows_in.at[step, most], sems.at[step]).wait()

    def in_group(i):
        return my_group * 8 + (my_row + i) % 8

    def across(i):
        return ((my_group + i) % 8) * 8 + my_row

    for load in loads[1:5]:
        load.wait()
    for j in range(WIDTH // LANES):
        gated = key[:, columns(j)].astype(jnp.float32) * value[:, columns(j)].astype(jnp.float32)
        conv_grad = grads[:, columns(j)].astype(jnp.float32) * query[:, columns(j)].astype(jnp.float32)
        rows_out[j] = jnp.sum(gated * conv_grad, axis=0, keepdims=True)
    send_rows(0, lambda i: rows_out.at[(my_row + i) % 8], in_group, my_row)
    rows_in[0, pl.ds(my_row, 1)] = rows_out[pl.ds(my_row, 1)]

    for j in range(WIDTH // LANES):
        gated = key[:, columns(j)].astype(jnp.float32) * value[:, columns(j)].astype(jnp.float32)
        leaving[1, columns(j), :] = gated.T
    send_signal(1)

    for j in range(WIDTH // LANES):
        conv_grad = grads[:, columns(j)].astype(jnp.float32) * query[:, columns(j)].astype(jnp.float32)
        leaving[2, columns(j), :] = conv_grad.T
    send_signal(2)

    for load in loads[5:]:
        load.wait()

    def forward(s):
        signal = landed.at[s]
        cos_twist, sin_twist = twists[0:HALF, :], twists[HALF:, :]
        for group in range(OWN // GROUP):
            lines = []
            for pair in range(GROUP // 2):
                first = group * GROUP + 2 * pair
                both = jnp.concatenate(
                    [signal[pl.ds(first + i, BLOCKS, stride=OWN), :] for i in range(2)], axis=1
                )
                parts = dot(mats[FWD_BLOCK, 0:BLOCKS], both)
                for i in range(2):
                    real, imag = parts[:HALF, columns(i)], parts[HALF:, columns(i)]
                    lines.append(
                        jnp.concatenate(
                            [real * cos_twist + imag * sin_twist, imag * cos_twist - real * sin_twist],
                            axis=1,
                        )
                    )
            spectra[s, group * ROWS : (group + 1) * ROWS, :] = dot(
                jnp.concatenate(lines, axis=0), mats[FWD_LOCAL, :]
            )

    def inverse(s, left, right, conjugate):
        result = leaving.at[3 + s]
        cos_twist, sin_twist = twists[0:HALF, :], twists[HALF:, :]
        for group in range(OWN // GROUP):
            rows = slice(group * ROWS, (group + 1) * ROWS)
            a_re, a_im = spectra[left, rows, 0:LANES], spectra[left, rows, LANES:]
            b_re, b_im = spectra[right, rows, 0:LANES], spectra[right, rows, LANES:]
            if conjugate:
                product = [a_re * b_re + a_im * b_im, a_re * b_im - a_im * b_re]
            else:
                product = [a_re * b_re - a_im * b_im, a_re * b_im + a_im * b_re]
            back = dot(jnp.concatenate(product, axis=1), mats[INV_LOCAL, :])
            for pair in range(GROUP // 2):
                pieces = []
                for i in range(2):
                    top = (2 * pair + i) * HALF
                    real, imag = back[top : top + HALF, 0:LANES], back[top : top + HALF, LANES:]
                    pieces.append(
                        jnp.concatenate(
                            [real * cos_twist - imag * sin_twist, real * sin_twist + imag * cos_twist],
                            axis=0,
                        )
                    )
                values = dot(mats[INV_BLOCK, 0 : 2 * HALF], jnp.concatenate(pieces, axis=1))
                first = group * GROUP + 2 * pair
                for i in range(2):
                    result[pl.ds(first + i, BLOCKS, stride=OWN), :] = values[:, columns(i)]

    wait_bytes(0, recv_sems)
    forward(0)
    wait_rows(0, row_recv_sems)
    rows_out[8] = jnp.sum(rows_in[0], axis=0)
    send_rows(1, lambda i: rows_out.at[8], across, my_group)
    rows_in[1, pl.ds(my_group, 1)] = rows_out[pl.ds(8, 1)]

    wait_bytes(1, recv_sems)
    forward(1)
    inverse(0, 0, 1, False)
    send_signal(3)

    wait_bytes(2, recv_sems)
    wait_rows(1, row_recv_sems)
    rows_out[9] = jnp.sum(rows_in[1], axis=0) * root_scale
    send_rows(2, lambda i: rows_out.at[9], in_group, my_row)
    rows_in[2, pl.ds(my_row, 1)] = rows_out[pl.ds(9, 1)]
    forward(2)
    inverse(1, 0, 2, True)
    send_signal(4)
    inverse(2, 1, 2, True)
    send_signal(5)

    wait_bytes(3, recv_sems)
    for j in range(WIDTH // LANES):
        gated = key[:, columns(j)].astype(jnp.float32) * value[:, columns(j)].astype(jnp.float32)
        conv = landed[3, columns(j), :].T + skip[:, columns(j)] * gated
        gq[:, columns(j)] = (grads[:, columns(j)].astype(jnp.float32) * conv).astype(jnp.bfloat16)
    wait_rows(2, row_recv_sems)
    for j in range(8):
        gs[j : j + 1, :] = rows_in[2, j]

    wait_bytes(4, recv_sems)
    for j in range(WIDTH // LANES):
        conv_grad = grads[:, columns(j)].astype(jnp.float32) * query[:, columns(j)].astype(jnp.float32)
        back = landed[4, columns(j), :].T + skip[:, columns(j)] * conv_grad
        gk[:, columns(j)] = (back * value[:, columns(j)].astype(jnp.float32)).astype(jnp.bfloat16)
        gv[:, columns(j)] = (back * key[:, columns(j)].astype(jnp.float32)).astype(jnp.bfloat16)

    wait_bytes(5, recv_sems)
    for j in range(WIDTH // LANES):
        gf[:, columns(j)] = landed[5, columns(j), :].T * root_scale

    for s in range(6):
        wait_bytes(s, send_sems)
    for step in range(3):
        wait_rows(step, row_send_sems)


def hand_over(*refs):
    given, taken, sems = refs[:5], refs[5:10], refs[10]
    writes = [pltpu.make_async_copy(given[i], taken[i], sems.at[i]) for i in range(5)]
    for write in writes:
        write.start()
    for write in writes:
        write.wait()


def on_device(query_gate, key_gate, value_gate, out_grad, filter_taps, skip):
    matrices, twists = tables()
    shape = query_gate.shape
    assert shape == (LANES, WIDTH) and lax.axis_size("ctx") == BLOCKS
    bf16, f32 = jnp.bfloat16, jnp.float32
    out_shape = [
        jax.ShapeDtypeStruct(shape, bf16),
        jax.ShapeDtypeStruct(shape, bf16),
        jax.ShapeDtypeStruct(shape, bf16),
        jax.ShapeDtypeStruct(shape, f32),
        jax.ShapeDtypeStruct((8, LANES), f32),
    ]
    outs = pl.pallas_call(
        kernel,
        out_shape=[pltpu.VMEM(out.shape, out.dtype) for out in out_shape],
        in_specs=[pl.BlockSpec(memory_space=pl.ANY)] * 8,
        out_specs=[pl.BlockSpec(memory_space=pltpu.VMEM)] * 5,
        scratch_shapes=[
            *[pltpu.VMEM(shape, bf16)] * 4,
            pltpu.VMEM(shape, f32),
            pltpu.VMEM((1, WIDTH), f32),
            pltpu.VMEM(matrices.shape, f32),
            pltpu.VMEM(twists.shape, f32),
            pltpu.VMEM((6, WIDTH, LANES), f32),
            pltpu.VMEM((6, WIDTH, LANES), f32),
            pltpu.VMEM((3, OWN * HALF, 2 * LANES), f32),
            pltpu.VMEM((10, 1, LANES), f32),
            pltpu.VMEM((3, 8, 1, LANES), f32),
            pltpu.SemaphoreType.DMA((8,)),
            pltpu.SemaphoreType.DMA((6,)),
            pltpu.SemaphoreType.DMA((6,)),
            pltpu.SemaphoreType.DMA((3,)),
            pltpu.SemaphoreType.DMA((3,)),
        ],
        compiler_params=pltpu.CompilerParams(
            collective_id=0, has_side_effects=True, vmem_limit_bytes=40 << 20
        ),
        cost_estimate=pl.CostEstimate(
            flops=4 * 10**9, bytes_accessed=3 * 10**6, transcendentals=0
        ),
        name="hyena_backward",
    )(
        *[
            pltpu.with_memory_space_constraint(operand, pltpu.HBM)
            for operand in (
                query_gate, key_gate, value_gate, out_grad, filter_taps, skip.reshape(1, WIDTH),
                jnp.asarray(matrices), jnp.asarray(twists),
            )
        ]
    )
    outs = pl.pallas_call(
        hand_over,
        out_shape=[pltpu.HBM(out.shape, out.dtype) for out in out_shape],
        in_specs=[pl.BlockSpec(memory_space=pl.ANY)] * 5,
        out_specs=[pl.BlockSpec(memory_space=pl.ANY)] * 5,
        scratch_shapes=[pltpu.SemaphoreType.DMA((5,))],
        compiler_params=pltpu.CompilerParams(vmem_limit_bytes=8 << 20),
        cost_estimate=pl.CostEstimate(flops=0, bytes_accessed=3 * 10**6, transcendentals=0),
        name="hand_over",
    )(*[pltpu.with_memory_space_constraint(out, pltpu.VMEM) for out in outs])
    return (*outs[:4], outs[4].reshape(WIDTH))


def solution(mesh):
    return jax.shard_map(
        on_device,
        mesh=mesh,
        in_specs=(*[P("ctx", "dp")] * 5, P("dp")),
        out_specs=(*[P("ctx", "dp")] * 4, P("dp")),
        check_vma=False,
    )
```

```python
import functools
import math

import jax
import jax.numpy as jnp
import numpy as np
from jax import lax
from jax.experimental import pallas as pl
from jax.experimental.pallas import tpu as pltpu
from jax.sharding import PartitionSpec as P

MESH = pl.DeviceIdType.MESH
BLOCKS = 64
LANES = 128
WIDTH = 1024
OWN = WIDTH // BLOCKS
PERIOD = 2 * BLOCKS * LANES
HALF = 72
GROUP = 4
ROWS = GROUP * HALF
Z_ORDER = (4, 3, 5, 2, 6, 1, 7)


@functools.cache
def tables():
    k1 = np.arange(HALF)[:, None]
    valid = (k1 <= BLOCKS).astype(np.float64)
    block = np.arange(BLOCKS)[None, :]
    angle = 2 * np.pi * ((k1 * block) % (2 * BLOCKS)) / (2 * BLOCKS)
    fwd_block = np.concatenate([np.cos(angle) * valid, -np.sin(angle) * valid])
    fwd_block = np.pad(fwd_block, ((0, 0), (0, 256 - BLOCKS)))
    weight = np.where((k1 == 0) | (k1 == BLOCKS), 1.0, 2.0) * valid / PERIOD
    inv_block = np.concatenate([np.cos(angle) * weight, -np.sin(angle) * weight]).T
    inv_block = np.pad(inv_block, ((0, 0), (0, 256 - 2 * HALF)))
    ids = np.arange(LANES)
    local = 2 * np.pi * ((ids[:, None] * ids[None, :]) % LANES) / LANES
    cos, sin = np.cos(local), np.sin(local)
    fwd_local = np.block([[cos, -sin], [sin, cos]])
    inv_local = np.block([[cos, sin], [-sin, cos]])
    matrices = np.concatenate([fwd_block, fwd_local, inv_local, inv_block]).astype(np.float32)
    twist = 2 * np.pi * ((k1 * ids[None, :]) % PERIOD) / PERIOD
    twists = np.concatenate([np.cos(twist), np.sin(twist)]).astype(np.float32)
    return matrices, twists


FWD_BLOCK = slice(0, 2 * HALF)
FWD_LOCAL = slice(2 * HALF, 2 * HALF + 256)
INV_LOCAL = slice(2 * HALF + 256, 2 * HALF + 512)
INV_BLOCK = slice(2 * HALF + 512, 2 * HALF + 512 + BLOCKS)


def dot(left, right):
    return jnp.dot(
        left, right, precision=lax.Precision.HIGHEST, preferred_element_type=jnp.float32
    )


def kernel(
    query_hbm, key_hbm, value_hbm, grads_hbm, taps_hbm, skip_hbm, mats_hbm, twists_hbm,
    gq, gk, gv, gf, gs,
    query, key, value, grads, taps, skip, mats, twists,
    leaving, landed, spectra, rows_out, rows_in,
    load_sems, send_sems, recv_sems, row_send_sems, row_recv_sems, planes_in,
):
    me = lax.axis_index("ctx")
    dp = lax.axis_index("dp")
    my_x, my_z, my_y = me // 32, (me // 4) % 8, me % 4

    loads = [
        pltpu.make_async_copy(src, dst, load_sems.at[i])
        for i, (src, dst) in enumerate(
            ((taps_hbm, taps), (key_hbm, key), (value_hbm, value), (grads_hbm, grads),
             (query_hbm, query), (twists_hbm, twists), (mats_hbm, mats), (skip_hbm, skip))
        )
    ]
    loads[0].start()

    barrier = pltpu.get_barrier_semaphore()
    planes = [((my_z + dz) % 8) * 4 for dz in range(8)]
    spots = [((my_x + xy // 4) % 2) * 32 + (my_y + xy) % 4 for xy in range(8)]
    column = [planes[dz] + spots[0] for dz in Z_ORDER]
    plane = [planes[0] + spots[xy] for xy in (6, 5, 7, 4, 2, 1, 3)]
    for there in column + plane:
        pl.semaphore_signal(barrier, inc=1, device_id=(dp, there), device_id_type=MESH)
    for load in loads[1:]:
        load.start()

    def rows_of(device):
        return pl.ds(pl.multiple_of(device * OWN, OWN), OWN)

    def send_one(s, there):
        pltpu.make_async_remote_copy(
            src_ref=leaving.at[s, rows_of(there), :],
            dst_ref=landed.at[s, rows_of(me), :],
            send_sem=send_sems.at[s],
            recv_sem=recv_sems.at[s],
            device_id=(dp, there),
            device_id_type=MESH,
        ).start()

    def send_near(s):
        for there in column + plane:
            send_one(s, there)
        landed[s, rows_of(me), :] = leaving[s, rows_of(me), :]

    def send_far(s):
        def body(j, carry):
            for zi, dz in enumerate(Z_ORDER):
                xy = (j + zi) % 7 + 1
                spot = ((my_x + xy // 4) % 2) * 32 + (my_y + xy) % 4
                send_one(s, planes[dz] + spot)
            return carry

        lax.fori_loop(0, 7, body, 0)

    def send_signal(s):
        send_near(s)
        send_far(s)

    def wait_bytes(s, sems):
        most = pl.ds(0, (BLOCKS - 1) * OWN)
        pltpu.make_async_copy(leaving.at[s, most, :], landed.at[s, most, :], sems.at[s]).wait()

    def columns(j):
        return slice(j * LANES, (j + 1) * LANES)

    loads[0].wait()
    for j in range(WIDTH // LANES):
        leaving[0, columns(j), :] = taps[:, columns(j)].T
    pl.semaphore_wait(barrier, len(column) + len(plane))
    for there in column:
        pl.semaphore_signal(planes_in, inc=1, device_id=(dp, there), device_id_type=MESH)
    send_near(0)

    for load in loads[1:5]:
        load.wait()
    for j in range(WIDTH // LANES):
        gated = key[:, columns(j)].astype(jnp.float32) * value[:, columns(j)].astype(jnp.float32)
        leaving[1, columns(j), :] = gated.T
    send_near(1)
    for j in range(WIDTH // LANES):
        conv_grad = grads[:, columns(j)].astype(jnp.float32) * query[:, columns(j)].astype(jnp.float32)
        leaving[2, columns(j), :] = conv_grad.T
    send_near(2)

    my_row, my_group = me % 8, me // 8
    root_scale = 1.0 / math.sqrt(BLOCKS * LANES)

    def send_rows(step, source_of, device_of, slot):
        for i in range(1, 8):
            pltpu.make_async_remote_copy(
                src_ref=source_of(i),
                dst_ref=rows_in.at[step, slot],
                send_sem=row_send_sems.at[step],
                recv_sem=row_recv_sems.at[step],
                device_id=(dp, device_of(i)),
                device_id_type=MESH,
            ).start()

    def wait_rows(step, sems):
        most = pl.ds(0, 7)
        pltpu.make_async_copy(rows_in.at[step, most], rows_in.at[step, most], sems.at[step]).wait()

    def in_group(i):
        return my_group * 8 + (my_row + i) % 8

    def across(i):
        return ((my_group + i) % 8) * 8 + my_row

    for j in range(WIDTH // LANES):
        gated = key[:, columns(j)].astype(jnp.float32) * value[:, columns(j)].astype(jnp.float32)
        conv_grad = grads[:, columns(j)].astype(jnp.float32) * query[:, columns(j)].astype(jnp.float32)
        rows_out[j] = jnp.sum(gated * conv_grad, axis=0, keepdims=True)
    rows_in[0, pl.ds(my_row, 1)] = rows_out[pl.ds(my_row, 1)]

    pl.semaphore_wait(planes_in, len(column))
    send_far(0)
    send_rows(0, lambda i: rows_out.at[(my_row + i) % 8], in_group, my_row)
    send_far(1)
    send_far(2)

    for load in loads[5:]:
        load.wait()

    def forward(s):
        signal = landed.at[s]
        cos_twist, sin_twist = twists[0:HALF, :], twists[HALF:, :]
        for group in range(OWN // GROUP):
            lines = []
            for pair in range(GROUP // 2):
                first = group * GROUP + 2 * pair
                both = jnp.concatenate(
                    [signal[pl.ds(first + i, BLOCKS, stride=OWN), :] for i in range(2)], axis=1
                )
                parts = dot(mats[FWD_BLOCK, 0:BLOCKS], both)
                for i in range(2):
                    real, imag = parts[:HALF, columns(i)], parts[HALF:, columns(i)]
                    lines.append(
                        jnp.concatenate(
                            [real * cos_twist + imag * sin_twist, imag * cos_twist - real * sin_twist],
                            axis=1,
                        )
                    )
            spectra[s, group * ROWS : (group + 1) * ROWS, :] = dot(
                jnp.concatenate(lines, axis=0), mats[FWD_LOCAL, :]
            )

    def inverse(s, left, right, conjugate):
        result = leaving.at[3 + s]
        cos_twist, sin_twist = twists[0:HALF, :], twists[HALF:, :]
        for group in range(OWN // GROUP):
            rows = slice(group * ROWS, (group + 1) * ROWS)
            a_re, a_im = spectra[left, rows, 0:LANES], spectra[left, rows, LANES:]
            b_re, b_im = spectra[right, rows, 0:LANES], spectra[right, rows, LANES:]
            if conjugate:
                product = [a_re * b_re + a_im * b_im, a_re * b_im - a_im * b_re]
            else:
                product = [a_re * b_re - a_im * b_im, a_re * b_im + a_im * b_re]
            back = dot(jnp.concatenate(product, axis=1), mats[INV_LOCAL, :])
            for pair in range(GROUP // 2):
                pieces = []
                for i in range(2):
                    top = (2 * pair + i) * HALF
                    real, imag = back[top : top + HALF, 0:LANES], back[top : top + HALF, LANES:]
                    pieces.append(
                        jnp.concatenate(
                            [real * cos_twist - imag * sin_twist, real * sin_twist + imag * cos_twist],
                            axis=0,
                        )
                    )
                values = dot(mats[INV_BLOCK, 0 : 2 * HALF], jnp.concatenate(pieces, axis=1))
                first = group * GROUP + 2 * pair
                for i in range(2):
                    result[pl.ds(first + i, BLOCKS, stride=OWN), :] = values[:, columns(i)]

    wait_bytes(0, recv_sems)
    forward(0)
    wait_rows(0, row_recv_sems)
    rows_out[8] = jnp.sum(rows_in[0], axis=0)
    send_rows(1, lambda i: rows_out.at[8], across, my_group)
    rows_in[1, pl.ds(my_group, 1)] = rows_out[pl.ds(8, 1)]

    wait_bytes(1, recv_sems)
    forward(1)
    inverse(0, 0, 1, False)
    send_signal(3)

    wait_bytes(2, recv_sems)
    wait_rows(1, row_recv_sems)
    rows_out[9] = jnp.sum(rows_in[1], axis=0) * root_scale
    send_rows(2, lambda i: rows_out.at[9], in_group, my_row)
    rows_in[2, pl.ds(my_row, 1)] = rows_out[pl.ds(9, 1)]
    forward(2)
    inverse(1, 0, 2, True)
    send_signal(4)
    inverse(2, 1, 2, True)
    send_signal(5)

    wait_bytes(3, recv_sems)
    for j in range(WIDTH // LANES):
        gated = key[:, columns(j)].astype(jnp.float32) * value[:, columns(j)].astype(jnp.float32)
        conv = landed[3, columns(j), :].T + skip[:, columns(j)] * gated
        gq[:, columns(j)] = (grads[:, columns(j)].astype(jnp.float32) * conv).astype(jnp.bfloat16)
    wait_rows(2, row_recv_sems)
    for j in range(8):
        gs[j : j + 1, :] = rows_in[2, j]

    wait_bytes(4, recv_sems)
    for j in range(WIDTH // LANES):
        conv_grad = grads[:, columns(j)].astype(jnp.float32) * query[:, columns(j)].astype(jnp.float32)
        back = landed[4, columns(j), :].T + skip[:, columns(j)] * conv_grad
        gk[:, columns(j)] = (back * value[:, columns(j)].astype(jnp.float32)).astype(jnp.bfloat16)
        gv[:, columns(j)] = (back * key[:, columns(j)].astype(jnp.float32)).astype(jnp.bfloat16)

    wait_bytes(5, recv_sems)
    for j in range(WIDTH // LANES):
        gf[:, columns(j)] = landed[5, columns(j), :].T * root_scale

    for s in range(6):
        wait_bytes(s, send_sems)
    for step in range(3):
        wait_rows(step, row_send_sems)


def hand_over(*refs):
    given, taken, sems = refs[:5], refs[5:10], refs[10]
    writes = [pltpu.make_async_copy(given[i], taken[i], sems.at[i]) for i in range(5)]
    for write in writes:
        write.start()
    for write in writes:
        write.wait()


def on_device(query_gate, key_gate, value_gate, out_grad, filter_taps, skip):
    matrices, twists = tables()
    shape = query_gate.shape
    assert shape == (LANES, WIDTH) and lax.axis_size("ctx") == BLOCKS
    bf16, f32 = jnp.bfloat16, jnp.float32
    out_shape = [
        jax.ShapeDtypeStruct(shape, bf16),
        jax.ShapeDtypeStruct(shape, bf16),
        jax.ShapeDtypeStruct(shape, bf16),
        jax.ShapeDtypeStruct(shape, f32),
        jax.ShapeDtypeStruct((8, LANES), f32),
    ]
    outs = pl.pallas_call(
        kernel,
        out_shape=[pltpu.VMEM(out.shape, out.dtype) for out in out_shape],
        in_specs=[pl.BlockSpec(memory_space=pl.ANY)] * 8,
        out_specs=[pl.BlockSpec(memory_space=pltpu.VMEM)] * 5,
        scratch_shapes=[
            *[pltpu.VMEM(shape, bf16)] * 4,
            pltpu.VMEM(shape, f32),
            pltpu.VMEM((1, WIDTH), f32),
            pltpu.VMEM(matrices.shape, f32),
            pltpu.VMEM(twists.shape, f32),
            pltpu.VMEM((6, WIDTH, LANES), f32),
            pltpu.VMEM((6, WIDTH, LANES), f32),
            pltpu.VMEM((3, OWN * HALF, 2 * LANES), f32),
            pltpu.VMEM((10, 1, LANES), f32),
            pltpu.VMEM((3, 8, 1, LANES), f32),
            pltpu.SemaphoreType.DMA((8,)),
            pltpu.SemaphoreType.DMA((6,)),
            pltpu.SemaphoreType.DMA((6,)),
            pltpu.SemaphoreType.DMA((3,)),
            pltpu.SemaphoreType.DMA((3,)),
            pltpu.SemaphoreType.REGULAR,
        ],
        compiler_params=pltpu.CompilerParams(
            collective_id=0, has_side_effects=True, vmem_limit_bytes=40 << 20
        ),
        cost_estimate=pl.CostEstimate(
            flops=4 * 10**9, bytes_accessed=3 * 10**6, transcendentals=0
        ),
        name="hyena_backward",
    )(
        *[
            pltpu.with_memory_space_constraint(operand, pltpu.HBM)
            for operand in (
                query_gate, key_gate, value_gate, out_grad, filter_taps, skip.reshape(1, WIDTH),
                jnp.asarray(matrices), jnp.asarray(twists),
            )
        ]
    )
    outs = pl.pallas_call(
        hand_over,
        out_shape=[pltpu.HBM(out.shape, out.dtype) for out in out_shape],
        in_specs=[pl.BlockSpec(memory_space=pl.ANY)] * 5,
        out_specs=[pl.BlockSpec(memory_space=pl.ANY)] * 5,
        scratch_shapes=[pltpu.SemaphoreType.DMA((5,))],
        compiler_params=pltpu.CompilerParams(vmem_limit_bytes=8 << 20),
        cost_estimate=pl.CostEstimate(flops=0, bytes_accessed=3 * 10**6, transcendentals=0),
        name="hand_over",
    )(*[pltpu.with_memory_space_constraint(out, pltpu.VMEM) for out in outs])
    return (*outs[:4], outs[4].reshape(WIDTH))


def solution(mesh):
    return jax.shard_map(
        on_device,
        mesh=mesh,
        in_specs=(*[P("ctx", "dp")] * 5, P("dp")),
        out_specs=(*[P("ctx", "dp")] * 4, P("dp")),
        check_vma=False,
    )
```

```python
import functools
import math

import jax
import jax.numpy as jnp
import numpy as np
from jax import lax
from jax.experimental import pallas as pl
from jax.experimental.pallas import tpu as pltpu
from jax.sharding import PartitionSpec as P

MESH = pl.DeviceIdType.MESH
BLOCKS = 64
LANES = 128
WIDTH = 1024
OWN = WIDTH // BLOCKS
PERIOD = 2 * BLOCKS * LANES
HALF = 72
GROUP = 4
ROWS = GROUP * HALF
Z_ORDER = (4, 3, 5, 2, 6, 1, 7)
LATE_Y = 3


@functools.cache
def tables():
    k1 = np.arange(HALF)[:, None]
    valid = (k1 <= BLOCKS).astype(np.float64)
    block = np.arange(BLOCKS)[None, :]
    angle = 2 * np.pi * ((k1 * block) % (2 * BLOCKS)) / (2 * BLOCKS)
    fwd_block = np.concatenate([np.cos(angle) * valid, -np.sin(angle) * valid])
    fwd_block = np.pad(fwd_block, ((0, 0), (0, 256 - BLOCKS)))
    weight = np.where((k1 == 0) | (k1 == BLOCKS), 1.0, 2.0) * valid / PERIOD
    inv_block = np.concatenate([np.cos(angle) * weight, -np.sin(angle) * weight]).T
    inv_block = np.pad(inv_block, ((0, 0), (0, 256 - 2 * HALF)))
    ids = np.arange(LANES)
    local = 2 * np.pi * ((ids[:, None] * ids[None, :]) % LANES) / LANES
    cos, sin = np.cos(local), np.sin(local)
    fwd_local = np.block([[cos, -sin], [sin, cos]])
    inv_local = np.block([[cos, sin], [-sin, cos]])
    matrices = np.concatenate([fwd_block, fwd_local, inv_local, inv_block]).astype(np.float32)
    twist = 2 * np.pi * ((k1 * ids[None, :]) % PERIOD) / PERIOD
    twists = np.concatenate([np.cos(twist), np.sin(twist)]).astype(np.float32)
    return matrices, twists


FWD_BLOCK = slice(0, 2 * HALF)
FWD_LOCAL = slice(2 * HALF, 2 * HALF + 256)
INV_LOCAL = slice(2 * HALF + 256, 2 * HALF + 512)
INV_BLOCK = slice(2 * HALF + 512, 2 * HALF + 512 + BLOCKS)


def dot(left, right):
    return jnp.dot(
        left, right, precision=lax.Precision.HIGHEST, preferred_element_type=jnp.float32
    )


def kernel(
    query_hbm, key_hbm, value_hbm, grads_hbm, taps_hbm, skip_hbm, mats_hbm, twists_hbm,
    gq, gk, gv, gf, gs,
    query, key, value, grads, taps, skip, mats, twists,
    leaving, landed, spectra, rows_out, rows_in,
    load_sems, send_sems, recv_sems, row_send_sems, row_recv_sems, planes_in,
):
    me = lax.axis_index("ctx")
    dp = lax.axis_index("dp")
    my_x, my_z, my_y = me // 32, (me // 4) % 8, me % 4

    loads = [
        pltpu.make_async_copy(src, dst, load_sems.at[i])
        for i, (src, dst) in enumerate(
            ((taps_hbm, taps), (key_hbm, key), (value_hbm, value), (grads_hbm, grads),
             (query_hbm, query), (twists_hbm, twists), (mats_hbm, mats), (skip_hbm, skip))
        )
    ]
    loads[0].start()

    barrier = pltpu.get_barrier_semaphore()
    planes = [((my_z + dz) % 8) * 4 for dz in range(8)]
    spots = [((my_x + xy // 4) % 2) * 32 + (my_y + xy) % 4 for xy in range(8)]
    column = [planes[dz] + spots[0] for dz in Z_ORDER]
    plane = [planes[0] + spots[xy] for xy in (6, 5, 7, 4, 2, 1, 3)]
    for there in column + plane:
        pl.semaphore_signal(barrier, inc=1, device_id=(dp, there), device_id_type=MESH)
    for load in loads[1:]:
        load.start()

    def rows_of(device):
        return pl.ds(pl.multiple_of(device * OWN, OWN), OWN)

    def send_one(s, there):
        pltpu.make_async_remote_copy(
            src_ref=leaving.at[s, rows_of(there), :],
            dst_ref=landed.at[s, rows_of(me), :],
            send_sem=send_sems.at[s],
            recv_sem=recv_sems.at[s],
            device_id=(dp, there),
            device_id_type=MESH,
        ).start()

    def send_near(s):
        for there in column + plane:
            send_one(s, there)
        landed[s, rows_of(me), :] = leaving[s, rows_of(me), :]

    def send_far(s):
        def body(j, carry):
            for zi, dz in enumerate(Z_ORDER):
                xy = (j + zi) % 7 + 1
                spot = ((my_x + xy // 4) % 2) * 32 + (my_y + xy) % 4
                send_one(s, planes[dz] + spot)
            return carry

        lax.fori_loop(0, 7, body, 0)

    def send_signal(s):
        send_near(s)
        send_far(s)

    def send_last(s):
        def early(j, carry):
            for zi, dz in enumerate((*Z_ORDER, 0)):
                xy = (j + zi) % 8
                x, y = (my_x + xy // 4) % 2, (my_y + xy) % 4
                there = x * 32 + planes[dz] + y

                @pl.when((there != me) & ((x == 0) | (y < LATE_Y)))
                def _():
                    send_one(s, there)

            return carry

        def late(j, carry):
            for zi, dz in enumerate((*Z_ORDER, 0)):
                there = 32 + planes[dz] + LATE_Y + (j + zi) % (4 - LATE_Y)

                @pl.when(there != me)
                def _():
                    send_one(s, there)

            return carry

        lax.fori_loop(0, 8, early, 0)
        lax.fori_loop(0, 4 - LATE_Y, late, 0)
        landed[s, rows_of(me), :] = leaving[s, rows_of(me), :]

    def wait_bytes(s, sems):
        most = pl.ds(0, (BLOCKS - 1) * OWN)
        pltpu.make_async_copy(leaving.at[s, most, :], landed.at[s, most, :], sems.at[s]).wait()

    def columns(j):
        return slice(j * LANES, (j + 1) * LANES)

    loads[0].wait()
    for j in range(WIDTH // LANES):
        leaving[0, columns(j), :] = taps[:, columns(j)].T
    pl.semaphore_wait(barrier, len(column) + len(plane))
    for there in column:
        pl.semaphore_signal(planes_in, inc=1, device_id=(dp, there), device_id_type=MESH)
    send_near(0)

    for load in loads[1:5]:
        load.wait()
    for j in range(WIDTH // LANES):
        gated = key[:, columns(j)].astype(jnp.float32) * value[:, columns(j)].astype(jnp.float32)
        leaving[1, columns(j), :] = gated.T
    send_near(1)
    for j in range(WIDTH // LANES):
        conv_grad = grads[:, columns(j)].astype(jnp.float32) * query[:, columns(j)].astype(jnp.float32)
        leaving[2, columns(j), :] = conv_grad.T
    send_near(2)

    my_row, my_group = me % 8, me // 8
    root_scale = 1.0 / math.sqrt(BLOCKS * LANES)

    def send_rows(step, source_of, device_of, slot):
        for i in range(1, 8):
            pltpu.make_async_remote_copy(
                src_ref=source_of(i),
                dst_ref=rows_in.at[step, slot],
                send_sem=row_send_sems.at[step],
                recv_sem=row_recv_sems.at[step],
                device_id=(dp, device_of(i)),
                device_id_type=MESH,
            ).start()

    def wait_rows(step, sems):
        most = pl.ds(0, 7)
        pltpu.make_async_copy(rows_in.at[step, most], rows_in.at[step, most], sems.at[step]).wait()

    def in_group(i):
        return my_group * 8 + (my_row + i) % 8

    def across(i):
        return ((my_group + i) % 8) * 8 + my_row

    for j in range(WIDTH // LANES):
        gated = key[:, columns(j)].astype(jnp.float32) * value[:, columns(j)].astype(jnp.float32)
        conv_grad = grads[:, columns(j)].astype(jnp.float32) * query[:, columns(j)].astype(jnp.float32)
        rows_out[j] = jnp.sum(gated * conv_grad, axis=0, keepdims=True)
    rows_in[0, pl.ds(my_row, 1)] = rows_out[pl.ds(my_row, 1)]

    pl.semaphore_wait(planes_in, len(column))
    send_far(0)
    send_rows(0, lambda i: rows_out.at[(my_row + i) % 8], in_group, my_row)
    send_far(1)
    send_far(2)

    for load in loads[5:]:
        load.wait()

    def forward(s):
        signal = landed.at[s]
        cos_twist, sin_twist = twists[0:HALF, :], twists[HALF:, :]
        for group in range(OWN // GROUP):
            lines = []
            for pair in range(GROUP // 2):
                first = group * GROUP + 2 * pair
                both = jnp.concatenate(
                    [signal[pl.ds(first + i, BLOCKS, stride=OWN), :] for i in range(2)], axis=1
                )
                parts = dot(mats[FWD_BLOCK, 0:BLOCKS], both)
                for i in range(2):
                    real, imag = parts[:HALF, columns(i)], parts[HALF:, columns(i)]
                    lines.append(
                        jnp.concatenate(
                            [real * cos_twist + imag * sin_twist, imag * cos_twist - real * sin_twist],
                            axis=1,
                        )
                    )
            spectra[s, group * ROWS : (group + 1) * ROWS, :] = dot(
                jnp.concatenate(lines, axis=0), mats[FWD_LOCAL, :]
            )

    def inverse(s, left, right, conjugate):
        result = leaving.at[3 + s]
        cos_twist, sin_twist = twists[0:HALF, :], twists[HALF:, :]
        for group in range(OWN // GROUP):
            rows = slice(group * ROWS, (group + 1) * ROWS)
            a_re, a_im = spectra[left, rows, 0:LANES], spectra[left, rows, LANES:]
            b_re, b_im = spectra[right, rows, 0:LANES], spectra[right, rows, LANES:]
            if conjugate:
                product = [a_re * b_re + a_im * b_im, a_re * b_im - a_im * b_re]
            else:
                product = [a_re * b_re - a_im * b_im, a_re * b_im + a_im * b_re]
            back = dot(jnp.concatenate(product, axis=1), mats[INV_LOCAL, :])
            for pair in range(GROUP // 2):
                pieces = []
                for i in range(2):
                    top = (2 * pair + i) * HALF
                    real, imag = back[top : top + HALF, 0:LANES], back[top : top + HALF, LANES:]
                    pieces.append(
                        jnp.concatenate(
                            [real * cos_twist - imag * sin_twist, real * sin_twist + imag * cos_twist],
                            axis=0,
                        )
                    )
                values = dot(mats[INV_BLOCK, 0 : 2 * HALF], jnp.concatenate(pieces, axis=1))
                first = group * GROUP + 2 * pair
                for i in range(2):
                    result[pl.ds(first + i, BLOCKS, stride=OWN), :] = values[:, columns(i)]

    wait_bytes(0, recv_sems)
    forward(0)
    wait_rows(0, row_recv_sems)
    rows_out[8] = jnp.sum(rows_in[0], axis=0)
    send_rows(1, lambda i: rows_out.at[8], across, my_group)
    rows_in[1, pl.ds(my_group, 1)] = rows_out[pl.ds(8, 1)]

    wait_bytes(1, recv_sems)
    forward(1)
    inverse(0, 0, 1, False)
    send_signal(3)

    wait_bytes(2, recv_sems)
    wait_rows(1, row_recv_sems)
    rows_out[9] = jnp.sum(rows_in[1], axis=0) * root_scale
    send_rows(2, lambda i: rows_out.at[9], in_group, my_row)
    rows_in[2, pl.ds(my_row, 1)] = rows_out[pl.ds(9, 1)]
    forward(2)
    inverse(1, 0, 2, True)
    send_signal(4)
    inverse(2, 1, 2, True)
    send_last(5)

    wait_bytes(3, recv_sems)
    for j in range(WIDTH // LANES):
        gated = key[:, columns(j)].astype(jnp.float32) * value[:, columns(j)].astype(jnp.float32)
        conv = landed[3, columns(j), :].T + skip[:, columns(j)] * gated
        gq[:, columns(j)] = (grads[:, columns(j)].astype(jnp.float32) * conv).astype(jnp.bfloat16)
    wait_rows(2, row_recv_sems)
    for j in range(8):
        gs[j : j + 1, :] = rows_in[2, j]

    wait_bytes(4, recv_sems)
    for j in range(WIDTH // LANES):
        conv_grad = grads[:, columns(j)].astype(jnp.float32) * query[:, columns(j)].astype(jnp.float32)
        back = landed[4, columns(j), :].T + skip[:, columns(j)] * conv_grad
        gk[:, columns(j)] = (back * value[:, columns(j)].astype(jnp.float32)).astype(jnp.bfloat16)
        gv[:, columns(j)] = (back * key[:, columns(j)].astype(jnp.float32)).astype(jnp.bfloat16)

    wait_bytes(5, recv_sems)
    for j in range(WIDTH // LANES):
        gf[:, columns(j)] = landed[5, columns(j), :].T * root_scale

    for s in range(6):
        wait_bytes(s, send_sems)
    for step in range(3):
        wait_rows(step, row_send_sems)


def hand_over(*refs):
    given, taken, sems = refs[:5], refs[5:10], refs[10]
    writes = [pltpu.make_async_copy(given[i], taken[i], sems.at[i]) for i in range(5)]
    for write in writes:
        write.start()
    for write in writes:
        write.wait()


def on_device(query_gate, key_gate, value_gate, out_grad, filter_taps, skip):
    matrices, twists = tables()
    shape = query_gate.shape
    assert shape == (LANES, WIDTH) and lax.axis_size("ctx") == BLOCKS
    bf16, f32 = jnp.bfloat16, jnp.float32
    out_shape = [
        jax.ShapeDtypeStruct(shape, bf16),
        jax.ShapeDtypeStruct(shape, bf16),
        jax.ShapeDtypeStruct(shape, bf16),
        jax.ShapeDtypeStruct(shape, f32),
        jax.ShapeDtypeStruct((8, LANES), f32),
    ]
    outs = pl.pallas_call(
        kernel,
        out_shape=[pltpu.VMEM(out.shape, out.dtype) for out in out_shape],
        in_specs=[pl.BlockSpec(memory_space=pl.ANY)] * 8,
        out_specs=[pl.BlockSpec(memory_space=pltpu.VMEM)] * 5,
        scratch_shapes=[
            *[pltpu.VMEM(shape, bf16)] * 4,
            pltpu.VMEM(shape, f32),
            pltpu.VMEM((1, WIDTH), f32),
            pltpu.VMEM(matrices.shape, f32),
            pltpu.VMEM(twists.shape, f32),
            pltpu.VMEM((6, WIDTH, LANES), f32),
            pltpu.VMEM((6, WIDTH, LANES), f32),
            pltpu.VMEM((3, OWN * HALF, 2 * LANES), f32),
            pltpu.VMEM((10, 1, LANES), f32),
            pltpu.VMEM((3, 8, 1, LANES), f32),
            pltpu.SemaphoreType.DMA((8,)),
            pltpu.SemaphoreType.DMA((6,)),
            pltpu.SemaphoreType.DMA((6,)),
            pltpu.SemaphoreType.DMA((3,)),
            pltpu.SemaphoreType.DMA((3,)),
            pltpu.SemaphoreType.REGULAR,
        ],
        compiler_params=pltpu.CompilerParams(
            collective_id=0, has_side_effects=True, vmem_limit_bytes=40 << 20
        ),
        cost_estimate=pl.CostEstimate(
            flops=4 * 10**9, bytes_accessed=3 * 10**6, transcendentals=0
        ),
        name="hyena_backward",
    )(
        *[
            pltpu.with_memory_space_constraint(operand, pltpu.HBM)
            for operand in (
                query_gate, key_gate, value_gate, out_grad, filter_taps, skip.reshape(1, WIDTH),
                jnp.asarray(matrices), jnp.asarray(twists),
            )
        ]
    )
    outs = pl.pallas_call(
        hand_over,
        out_shape=[pltpu.HBM(out.shape, out.dtype) for out in out_shape],
        in_specs=[pl.BlockSpec(memory_space=pl.ANY)] * 5,
        out_specs=[pl.BlockSpec(memory_space=pl.ANY)] * 5,
        scratch_shapes=[pltpu.SemaphoreType.DMA((5,))],
        compiler_params=pltpu.CompilerParams(vmem_limit_bytes=8 << 20),
        cost_estimate=pl.CostEstimate(flops=0, bytes_accessed=3 * 10**6, transcendentals=0),
        name="hand_over",
    )(*[pltpu.with_memory_space_constraint(out, pltpu.VMEM) for out in outs])
    return (*outs[:4], outs[4].reshape(WIDTH))


def solution(mesh):
    return jax.shard_map(
        on_device,
        mesh=mesh,
        in_specs=(*[P("ctx", "dp")] * 5, P("dp")),
        out_specs=(*[P("ctx", "dp")] * 4, P("dp")),
        check_vma=False,
    )
```

```python
import functools
import math

import jax
import jax.numpy as jnp
import numpy as np
from jax import lax
from jax.experimental import pallas as pl
from jax.experimental.pallas import tpu as pltpu
from jax.sharding import PartitionSpec as P

MESH = pl.DeviceIdType.MESH
BLOCKS = 64
LANES = 128
WIDTH = 1024
OWN = WIDTH // BLOCKS
PERIOD = 2 * BLOCKS * LANES
HALF = 72
GROUP = 4
ROWS = GROUP * HALF
Z_ORDER = (4, 3, 5, 2, 6, 1, 7)
LATE_Y = 3


@functools.cache
def tables():
    k1 = np.arange(HALF)[:, None]
    valid = (k1 <= BLOCKS).astype(np.float64)
    block = np.arange(BLOCKS)[None, :]
    angle = 2 * np.pi * ((k1 * block) % (2 * BLOCKS)) / (2 * BLOCKS)
    fwd_block = np.concatenate([np.cos(angle) * valid, -np.sin(angle) * valid])
    fwd_block = np.pad(fwd_block, ((0, 0), (0, 256 - BLOCKS)))
    weight = np.where((k1 == 0) | (k1 == BLOCKS), 1.0, 2.0) * valid / PERIOD
    inv_block = np.concatenate([np.cos(angle) * weight, -np.sin(angle) * weight]).T
    inv_block = np.pad(inv_block, ((0, 0), (0, 256 - 2 * HALF)))
    ids = np.arange(LANES)
    local = 2 * np.pi * ((ids[:, None] * ids[None, :]) % LANES) / LANES
    cos, sin = np.cos(local), np.sin(local)
    fwd_local = np.block([[cos, -sin], [sin, cos]])
    inv_local = np.block([[cos, sin], [-sin, cos]])
    matrices = np.concatenate([fwd_block, fwd_local, inv_local, inv_block]).astype(np.float32)
    twist = 2 * np.pi * ((k1 * ids[None, :]) % PERIOD) / PERIOD
    twists = np.concatenate([np.cos(twist), np.sin(twist)]).astype(np.float32)
    return matrices, twists


FWD_BLOCK = slice(0, 2 * HALF)
FWD_LOCAL = slice(2 * HALF, 2 * HALF + 256)
INV_LOCAL = slice(2 * HALF + 256, 2 * HALF + 512)
INV_BLOCK = slice(2 * HALF + 512, 2 * HALF + 512 + BLOCKS)


def dot(left, right):
    return jnp.dot(
        left, right, precision=lax.Precision.HIGHEST, preferred_element_type=jnp.float32
    )


def kernel(
    query_hbm, key_hbm, value_hbm, grads_hbm, taps_hbm, skip_hbm, mats_hbm, twists_hbm,
    gq, gk, gv, gf, gs,
    query, key, value, grads, taps, skip, mats, twists,
    leaving, landed, spectra, rows_out, rows_in,
    load_sems, send_sems, recv_sems, row_send_sems, row_recv_sems, planes_in,
):
    me = lax.axis_index("ctx")
    dp = lax.axis_index("dp")
    my_x, my_z, my_y = me // 32, (me // 4) % 8, me % 4

    loads = [
        pltpu.make_async_copy(src, dst, load_sems.at[i])
        for i, (src, dst) in enumerate(
            ((taps_hbm, taps), (key_hbm, key), (value_hbm, value), (grads_hbm, grads),
             (query_hbm, query), (twists_hbm, twists), (mats_hbm, mats), (skip_hbm, skip))
        )
    ]
    loads[0].start()

    barrier = pltpu.get_barrier_semaphore()
    planes = [((my_z + dz) % 8) * 4 for dz in range(8)]
    spots = [((my_x + xy // 4) % 2) * 32 + (my_y + xy) % 4 for xy in range(8)]
    column = [planes[dz] + spots[0] for dz in Z_ORDER]
    plane = [planes[0] + spots[xy] for xy in (6, 5, 7, 4, 2, 1, 3)]
    for there in column + plane:
        pl.semaphore_signal(barrier, inc=1, device_id=(dp, there), device_id_type=MESH)
    for load in loads[1:]:
        load.start()

    def rows_of(device):
        return pl.ds(pl.multiple_of(device * OWN, OWN), OWN)

    def send_one(s, there):
        pltpu.make_async_remote_copy(
            src_ref=leaving.at[s, rows_of(there), :],
            dst_ref=landed.at[s, rows_of(me), :],
            send_sem=send_sems.at[s],
            recv_sem=recv_sems.at[s],
            device_id=(dp, there),
            device_id_type=MESH,
        ).start()

    def send_near(s):
        for there in column + plane:
            send_one(s, there)
        landed[s, rows_of(me), :] = leaving[s, rows_of(me), :]

    def send_far(s):
        def body(j, carry):
            for zi, dz in enumerate(Z_ORDER):
                xy = (j + zi) % 7 + 1
                spot = ((my_x + xy // 4) % 2) * 32 + (my_y + xy) % 4
                send_one(s, planes[dz] + spot)
            return carry

        lax.fori_loop(0, 7, body, 0)

    def send_signal(s):
        send_near(s)
        send_far(s)

    def send_last(s):
        def early(j, carry):
            for zi, dz in enumerate((*Z_ORDER, 0)):
                xy = (j + zi) % 8
                x, y = (my_x + xy // 4) % 2, (my_y + xy) % 4
                there = x * 32 + planes[dz] + y

                @pl.when((there != me) & ((x == 0) | (y < LATE_Y)))
                def _():
                    send_one(s, there)

            return carry

        def late(j, carry):
            for zi, dz in enumerate((*Z_ORDER, 0)):
                there = 32 + planes[dz] + LATE_Y + (j + zi) % (4 - LATE_Y)

                @pl.when(there != me)
                def _():
                    send_one(s, there)

            return carry

        lax.fori_loop(0, 8, early, 0)
        lax.fori_loop(0, 4 - LATE_Y, late, 0)
        landed[s, rows_of(me), :] = leaving[s, rows_of(me), :]

    def wait_bytes(s, sems):
        most = pl.ds(0, (BLOCKS - 1) * OWN)
        pltpu.make_async_copy(leaving.at[s, most, :], landed.at[s, most, :], sems.at[s]).wait()

    def columns(j):
        return slice(j * LANES, (j + 1) * LANES)

    loads[0].wait()
    for j in range(WIDTH // LANES):
        leaving[0, columns(j), :] = taps[:, columns(j)].T
    pl.semaphore_wait(barrier, len(column) + len(plane))
    for there in column:
        pl.semaphore_signal(planes_in, inc=1, device_id=(dp, there), device_id_type=MESH)
    send_near(0)

    for load in loads[1:5]:
        load.wait()
    for j in range(WIDTH // LANES):
        gated = key[:, columns(j)].astype(jnp.float32) * value[:, columns(j)].astype(jnp.float32)
        leaving[1, columns(j), :] = gated.T
    send_near(1)
    for j in range(WIDTH // LANES):
        conv_grad = grads[:, columns(j)].astype(jnp.float32) * query[:, columns(j)].astype(jnp.float32)
        leaving[2, columns(j), :] = conv_grad.T
    send_near(2)

    my_row, my_group = me % 8, me // 8
    root_scale = 1.0 / math.sqrt(BLOCKS * LANES)

    def send_rows(step, source_of, device_of, slot):
        for i in range(1, 8):
            pltpu.make_async_remote_copy(
                src_ref=source_of(i),
                dst_ref=rows_in.at[step, slot],
                send_sem=row_send_sems.at[step],
                recv_sem=row_recv_sems.at[step],
                device_id=(dp, device_of(i)),
                device_id_type=MESH,
            ).start()

    def wait_rows(step, sems):
        most = pl.ds(0, 7)
        pltpu.make_async_copy(rows_in.at[step, most], rows_in.at[step, most], sems.at[step]).wait()

    def in_group(i):
        return my_group * 8 + (my_row + i) % 8

    def across(i):
        return ((my_group + i) % 8) * 8 + my_row

    for j in range(WIDTH // LANES):
        gated = key[:, columns(j)].astype(jnp.float32) * value[:, columns(j)].astype(jnp.float32)
        conv_grad = grads[:, columns(j)].astype(jnp.float32) * query[:, columns(j)].astype(jnp.float32)
        rows_out[j] = jnp.sum(gated * conv_grad, axis=0, keepdims=True)
    rows_in[0, pl.ds(my_row, 1)] = rows_out[pl.ds(my_row, 1)]

    pl.semaphore_wait(planes_in, len(column))
    send_far(0)
    send_rows(0, lambda i: rows_out.at[(my_row + i) % 8], in_group, my_row)
    send_far(1)
    send_far(2)

    for load in loads[5:]:
        load.wait()

    def forward(s):
        signal = landed.at[s]
        cos_twist, sin_twist = twists[0:HALF, :], twists[HALF:, :]
        for group in range(OWN // GROUP):
            lines = []
            for pair in range(GROUP // 2):
                first = group * GROUP + 2 * pair
                both = jnp.concatenate(
                    [signal[pl.ds(first + i, BLOCKS, stride=OWN), :] for i in range(2)], axis=1
                )
                parts = dot(mats[FWD_BLOCK, 0:BLOCKS], both)
                for i in range(2):
                    real, imag = parts[:HALF, columns(i)], parts[HALF:, columns(i)]
                    lines.append(
                        jnp.concatenate(
                            [real * cos_twist + imag * sin_twist, imag * cos_twist - real * sin_twist],
                            axis=1,
                        )
                    )
            spectra[s, group * ROWS : (group + 1) * ROWS, :] = dot(
                jnp.concatenate(lines, axis=0), mats[FWD_LOCAL, :]
            )

    def inverse(s, left, right, conjugate):
        result = leaving.at[3 + s]
        cos_twist, sin_twist = twists[0:HALF, :], twists[HALF:, :]
        for group in range(OWN // GROUP):
            rows = slice(group * ROWS, (group + 1) * ROWS)
            a_re, a_im = spectra[left, rows, 0:LANES], spectra[left, rows, LANES:]
            b_re, b_im = spectra[right, rows, 0:LANES], spectra[right, rows, LANES:]
            if conjugate:
                product = [a_re * b_re + a_im * b_im, a_re * b_im - a_im * b_re]
            else:
                product = [a_re * b_re - a_im * b_im, a_re * b_im + a_im * b_re]
            back = dot(jnp.concatenate(product, axis=1), mats[INV_LOCAL, :])
            for pair in range(GROUP // 2):
                pieces = []
                for i in range(2):
                    top = (2 * pair + i) * HALF
                    real, imag = back[top : top + HALF, 0:LANES], back[top : top + HALF, LANES:]
                    pieces.append(
                        jnp.concatenate(
                            [real * cos_twist - imag * sin_twist, real * sin_twist + imag * cos_twist],
                            axis=0,
                        )
                    )
                values = dot(mats[INV_BLOCK, 0 : 2 * HALF], jnp.concatenate(pieces, axis=1))
                first = group * GROUP + 2 * pair
                for i in range(2):
                    result[pl.ds(first + i, BLOCKS, stride=OWN), :] = values[:, columns(i)]

    wait_bytes(0, recv_sems)
    forward(0)
    wait_rows(0, row_recv_sems)
    rows_out[8] = jnp.sum(rows_in[0], axis=0)
    send_rows(1, lambda i: rows_out.at[8], across, my_group)
    rows_in[1, pl.ds(my_group, 1)] = rows_out[pl.ds(8, 1)]

    wait_bytes(1, recv_sems)
    forward(1)
    inverse(0, 0, 1, False)
    send_signal(3)

    wait_bytes(2, recv_sems)
    wait_rows(1, row_recv_sems)
    rows_out[9] = jnp.sum(rows_in[1], axis=0) * root_scale
    send_rows(2, lambda i: rows_out.at[9], in_group, my_row)
    rows_in[2, pl.ds(my_row, 1)] = rows_out[pl.ds(9, 1)]
    forward(2)
    inverse(1, 0, 2, True)
    send_signal(4)
    inverse(2, 1, 2, True)
    send_last(5)

    wait_bytes(3, recv_sems)
    for j in range(WIDTH // LANES):
        gated = key[:, columns(j)].astype(jnp.float32) * value[:, columns(j)].astype(jnp.float32)
        conv = landed[3, columns(j), :].T + skip[:, columns(j)] * gated
        gq[:, columns(j)] = (grads[:, columns(j)].astype(jnp.float32) * conv).astype(jnp.bfloat16)
    wait_rows(2, row_recv_sems)
    for j in range(8):
        gs[j : j + 1, :] = rows_in[2, j]

    wait_bytes(4, recv_sems)
    for j in range(WIDTH // LANES):
        conv_grad = grads[:, columns(j)].astype(jnp.float32) * query[:, columns(j)].astype(jnp.float32)
        back = landed[4, columns(j), :].T + skip[:, columns(j)] * conv_grad
        gk[:, columns(j)] = (back * value[:, columns(j)].astype(jnp.float32)).astype(jnp.bfloat16)
        gv[:, columns(j)] = (back * key[:, columns(j)].astype(jnp.float32)).astype(jnp.bfloat16)

    wait_bytes(5, recv_sems)
    for j in range(WIDTH // LANES):
        gf[:, columns(j)] = landed[5, columns(j), :].T * root_scale

    for s in range(6):
        wait_bytes(s, send_sems)
    for step in range(3):
        wait_rows(step, row_send_sems)


def hand_over(*refs):
    given, taken, sems = refs[:5], refs[5:10], refs[10]
    writes = [pltpu.make_async_copy(given[i], taken[i], sems.at[i]) for i in range(5)]
    for write in writes:
        write.start()
    for write in writes:
        write.wait()


def on_device(query_gate, key_gate, value_gate, out_grad, filter_taps, skip):
    matrices, twists = tables()
    shape = query_gate.shape
    assert shape == (LANES, WIDTH) and lax.axis_size("ctx") == BLOCKS
    bf16, f32 = jnp.bfloat16, jnp.float32
    out_shape = [
        jax.ShapeDtypeStruct(shape, bf16),
        jax.ShapeDtypeStruct(shape, bf16),
        jax.ShapeDtypeStruct(shape, bf16),
        jax.ShapeDtypeStruct(shape, f32),
        jax.ShapeDtypeStruct((8, LANES), f32),
    ]
    outs = pl.pallas_call(
        kernel,
        out_shape=[pltpu.VMEM(out.shape, out.dtype) for out in out_shape],
        in_specs=[pl.BlockSpec(memory_space=pl.ANY)] * 8,
        out_specs=[pl.BlockSpec(memory_space=pltpu.VMEM)] * 5,
        scratch_shapes=[
            *[pltpu.VMEM(shape, bf16)] * 4,
            pltpu.VMEM(shape, f32),
            pltpu.VMEM((1, WIDTH), f32),
            pltpu.VMEM(matrices.shape, f32),
            pltpu.VMEM(twists.shape, f32),
            pltpu.VMEM((6, WIDTH + OWN, LANES), f32),
            pltpu.VMEM((6, WIDTH + OWN, LANES), f32),
            pltpu.VMEM((3, OWN * HALF, 2 * LANES), f32),
            pltpu.VMEM((10, 1, LANES), f32),
            pltpu.VMEM((3, 8, 1, LANES), f32),
            pltpu.SemaphoreType.DMA((8,)),
            pltpu.SemaphoreType.DMA((6,)),
            pltpu.SemaphoreType.DMA((6,)),
            pltpu.SemaphoreType.DMA((3,)),
            pltpu.SemaphoreType.DMA((3,)),
            pltpu.SemaphoreType.REGULAR,
        ],
        compiler_params=pltpu.CompilerParams(
            collective_id=0, has_side_effects=True, vmem_limit_bytes=40 << 20
        ),
        cost_estimate=pl.CostEstimate(
            flops=4 * 10**9, bytes_accessed=3 * 10**6, transcendentals=0
        ),
        name="hyena_backward",
    )(
        *[
            pltpu.with_memory_space_constraint(operand, pltpu.HBM)
            for operand in (
                query_gate, key_gate, value_gate, out_grad, filter_taps, skip.reshape(1, WIDTH),
                jnp.asarray(matrices), jnp.asarray(twists),
            )
        ]
    )
    outs = pl.pallas_call(
        hand_over,
        out_shape=[pltpu.HBM(out.shape, out.dtype) for out in out_shape],
        in_specs=[pl.BlockSpec(memory_space=pl.ANY)] * 5,
        out_specs=[pl.BlockSpec(memory_space=pl.ANY)] * 5,
        scratch_shapes=[pltpu.SemaphoreType.DMA((5,))],
        compiler_params=pltpu.CompilerParams(vmem_limit_bytes=8 << 20),
        cost_estimate=pl.CostEstimate(flops=0, bytes_accessed=3 * 10**6, transcendentals=0),
        name="hand_over",
    )(*[pltpu.with_memory_space_constraint(out, pltpu.VMEM) for out in outs])
    return (*outs[:4], outs[4].reshape(WIDTH))


def solution(mesh):
    return jax.shard_map(
        on_device,
        mesh=mesh,
        in_specs=(*[P("ctx", "dp")] * 5, P("dp")),
        out_specs=(*[P("ctx", "dp")] * 4, P("dp")),
        check_vma=False,
    )
```
